32 devices in a mesh: section: 2 (over y), dp: 4 (over z), tensor: 4 (over x, core).
Axes of the slice: x: 2, y: 2, z: 4, core: 2. Of those that a mesh axis runs over, the one named last changes fastest.
Arguments:
- inputs: bfloat16 [4, 2048, 768], P(None, ('dp', 'tensor')), may hold values from -6 to 6
- cotangent: bfloat16 [4, 2048, 768], P(None, ('dp', 'tensor')), may hold values from -6 to 6
- seq_lengths: int32 [4, 4, 4], P('dp'), may hold values from 0 to 512, as said below
- w_attn: bfloat16 [2, 768, 3, 768], P('section', None, None, 'tensor'), may hold values from -0.21875 to 0.21875
- b_qv: bfloat16 [2, 2, 768], P('section', None, 'tensor'), may hold values from -3 to 3
- w_proj: bfloat16 [2, 768, 768], P('section', 'tensor'), may hold values from -0.875 to 0.875
- b_proj: bfloat16 [2, 768], P('section'), may hold values from -3 to 3
- w_fc: bfloat16 [2, 768, 3072], P('section', None, 'tensor'), may hold values from -0.21875 to 0.21875
- b_fc: bfloat16 [2, 3072], P('section', 'tensor'), may hold values from -3 to 3
- w_out: bfloat16 [2, 3072, 768], P('section', 'tensor'), may hold values from -0.109375 to 0.109375
- b_out: bfloat16 [2, 768], P('section'), may hold values from -3 to 3
- ln_gain: bfloat16 [2, 2, 768], P('section'), may hold values from 0.25 to 1.75
- ln_bias: bfloat16 [2, 2, 768], P('section'), may hold values from -2 to 2
Outputs:
- section_out: bfloat16 [2, 4, 2048, 768], P('section', None, ('dp', 'tensor'))
- input_grad: bfloat16 [2, 4, 2048, 768], P('section', None, ('dp', 'tensor'))
- grad_w_attn: float32 [2, 768, 3, 768], P('section', 'dp', None, 'tensor')
- grad_b_qv: float32 [2, 2, 768], P('section', None, 'tensor')
- grad_w_proj: float32 [2, 768, 768], P('section', 'tensor', 'dp')
- grad_b_proj: float32 [2, 768], P('section', ('dp', 'tensor'))
- grad_w_fc: float32 [2, 768, 3072], P('section', 'dp', 'tensor')
- grad_b_fc: float32 [2, 3072], P('section', 'tensor')
- grad_w_out: float32 [2, 3072, 768], P('section', 'tensor', 'dp')
- grad_b_out: float32 [2, 768], P('section', ('dp', 'tensor'))
- grad_ln_gain: float32 [2, 2, 768], P('section', None, ('dp', 'tensor'))
- grad_ln_bias: float32 [2, 2, 768], P('section', None, ('dp', 'tensor'))
The draws below stay inside these ranges and needn't reach their ends.
Inputs may be any that keep to these rules, and one draw needn't show every extreme that they name: seq_lengths[g, m, j] is the number of slots of the j-th sequence of micro-batch m on data group g; the sequences lie end to end from slot 0 and slots after them are padding; each (g, m) totals at most 512, and on every group some micro-batch is one sequence of 512 slots.
All inputs are finite; a program needn't handle non-finite values.
Results may differ from the reference program's by a relative error of at most 0.02.
Values may be sent and summed in bfloat16 or wider, within the bound.
No kernel may reach another device: no remote copies, remote signals or barrier semaphores. Data moves between devices by JAX's collectives and lax.ppermute only.
A program may use at most 128 MiB of HBM per device.

```python
import jax
import jax.numpy as jnp
from jax import lax

D = 768
HEADS = 12
HEAD_DIM = 64
FF = 3072
SLOTS = 512
MICRO = 4
SEQS = 4
TOKS = 2048
N_DP = 4


def draw_seq_lengths(key, part):
    key = jax.random.fold_in(key, 11)
    key_live, key_cut, key_full = jax.random.split(key, 3)
    filled = jax.random.randint(key_live, (N_DP, MICRO, 1), SLOTS * 3 // 10, SLOTS + 1)
    cuts = jax.random.randint(key_cut, (N_DP, MICRO, SEQS - 1), 0, SLOTS + 1)
    cuts = jnp.sort(jnp.minimum(cuts, filled), axis=-1)
    bounds = jnp.concatenate([jnp.zeros((N_DP, MICRO, 1), jnp.int32), cuts, filled], axis=-1)
    lengths = bounds[..., 1:] - bounds[..., :-1]
    chosen = jax.random.randint(key_full, (N_DP, 1), 0, MICRO)
    full_row = (jnp.arange(SEQS) == 0).astype(jnp.int32) * SLOTS
    is_full = (jnp.arange(MICRO)[None, :] == chosen)[..., None]
    return jnp.where(is_full, full_row[None, None, :], lengths).astype(jnp.int32)


def shard_levels(rng, extent, pieces, low, top_value):
    loudness, own = 1.0, jax.random.fold_in(rng, 6)
    for axis_at, shards_of in pieces:
        draws = jnp.exp(jax.random.uniform(jax.random.fold_in(own, axis_at), (shards_of,), jnp.float32, low / len(pieces), top_value / len(pieces)))
        loudness = loudness * jnp.repeat(draws, extent[axis_at] // shards_of).reshape([-1 if axis == axis_at else 1 for axis in range(len(extent))])
    return loudness


def bell_draw(key, shape, width, most, shards=(), kind=jnp.bfloat16):
    entries = jax.random.normal(key, shape, jnp.float32) * width
    if len(shards) > 0:
        entries = shard_levels(key, shape, shards, -0.22, 0.18) * entries
    return jnp.clip(entries, min=-most, max=most).astype(kind)


def setup_inputs(seed: int = 0) -> dict:
    arg_keys = jax.random.split(jax.random.key(seed), 14)
    return {
        "inputs": bell_draw(arg_keys[0], (MICRO, TOKS, D), 1.0, 6.0, ((1, 16),)),
        "cotangent": bell_draw(arg_keys[1], (MICRO, TOKS, D), 1.0, 6.0, ((1, 16),)),
        "seq_lengths": draw_seq_lengths(jax.random.fold_in(arg_keys[13], 71), 0),
        "w_attn": bell_draw(arg_keys[3], (2, D, 3, D), D ** -0.5, 0.21875, ((0, 2), (3, 4))),
        "b_qv": bell_draw(arg_keys[4], (2, 2, D), 0.5, 3.0, ((0, 2), (2, 4))),
        "w_proj": bell_draw(arg_keys[5], (2, D, D), (D // 16) ** -0.5, 0.875, ((0, 2), (1, 4))),
        "b_proj": bell_draw(arg_keys[6], (2, D), 0.5, 3.0, ((0, 2),)),
        "w_fc": bell_draw(arg_keys[7], (2, D, FF), D ** -0.5, 0.21875, ((0, 2), (2, 4))),
        "b_fc": bell_draw(arg_keys[8], (2, FF), 0.5, 3.0, ((0, 2), (1, 4))),
        "w_out": bell_draw(arg_keys[9], (2, FF, D), FF ** -0.5, 0.109375, ((0, 2), (1, 4))),
        "b_out": bell_draw(arg_keys[10], (2, D), 0.5, 3.0, ((0, 2),)),
        "ln_gain": jnp.clip(1.0 + 0.15 * jax.random.normal(arg_keys[11], (2, 2, D), jnp.float32), 0.25, 1.75).astype(jnp.bfloat16),
        "ln_bias": bell_draw(arg_keys[12], (2, 2, D), 0.3, 2.0, ((0, 2),)),
    }


@jax.custom_vjp
def low(v):
    return lax.optimization_barrier(v.astype(jnp.bfloat16)).astype(jnp.float32)

@jax.custom_vjp
def low_back(v):
    return v

def low_keep(v):
    return (low(v), None)

def low_pass(kept, grad):
    return (grad,)

def back_keep(v):
    return (v, None)

def back_low(kept, grad):
    return (low(grad),)
low.defvjp(low_keep, low_pass)
low_back.defvjp(back_keep, back_low)
HIGH = lax.Precision.HIGHEST

def layer_norm(rows, gain, shift):
    center = lax.optimization_barrier(jnp.mean(rows, axis=-1, keepdims=True))
    centred = rows - center
    variance = lax.optimization_barrier(jnp.mean(centred * centred, axis=-1, keepdims=True))
    return centred * lax.rsqrt(variance + 1e-05) * gain + shift

def segment_masks(lengths):
    ends = jnp.cumsum(lengths).astype(jnp.int32)
    position = jnp.arange(SLOTS, dtype=jnp.int32)
    segment = lax.optimization_barrier(jnp.sum((position[:, None] >= ends[None, :]).astype(jnp.int32), axis=1))
    live = (position < ends[-1]).astype(jnp.float32)
    allowed = (segment[:, None] == segment[None, :]) & (position[None, :] <= position[:, None])
    return (live, allowed)

def block(params, rows, live, allowed):
    w_attn, b_qv, w_proj, b_proj, w_fc, b_fc, w_out, b_out, ln_gain, ln_bias = params
    normed = low(layer_norm(rows, ln_gain[0], ln_bias[0]))
    bias_row = jnp.concatenate([b_qv[0], jnp.zeros_like(b_qv[0]), b_qv[1]])
    mixed = jnp.dot(normed, w_attn.reshape(D, 3 * D), precision=HIGH) + bias_row
    mixed = low_back(low(mixed))
    queries = mixed[:, :D].reshape(SLOTS, HEADS, HEAD_DIM)
    keys = mixed[:, D:2 * D].reshape(SLOTS, HEADS, HEAD_DIM)
    values = mixed[:, 2 * D:].reshape(SLOTS, HEADS, HEAD_DIM)
    scores = jnp.einsum('qhd,khd->hqk', queries, keys, precision=HIGH) * HEAD_DIM ** (-0.5)
    scores = jnp.where(allowed[None], low_back(scores), -1e+30)
    weights = low(jax.nn.softmax(scores, axis=-1))
    context = jnp.einsum('hqk,khd->qhd', weights, values, precision=HIGH).reshape(SLOTS, D)
    context = low_back(low(context))
    middle = rows + low_back(jnp.dot(context, w_proj, precision=HIGH) + b_proj)
    normed_two = low(layer_norm(middle, ln_gain[1], ln_bias[1]))
    hidden = low_back(jnp.dot(normed_two, w_fc, precision=HIGH) + b_fc)
    active = low(jax.nn.gelu(hidden, approximate=True))
    branch = low_back(jnp.dot(active, w_out, precision=HIGH) + b_out)
    return live[:, None] * (middle + branch)

def pair(section_params, block_in, delta, lengths):
    live, allowed = segment_masks(lengths)
    first = low(block(section_params[0], block_in, live, allowed))
    second_in = low_back(first + delta)
    second = low(block(section_params[1], second_in, live, allowed))
    return (first, second)

def reference(inputs, cotangent, seq_lengths, w_attn, b_qv, w_proj, b_proj, w_fc, b_fc, w_out, b_out, ln_gain, ln_bias):
    weights = tuple((a.astype(jnp.float32) for a in (w_attn, b_qv, w_proj, b_proj, w_fc, b_fc, w_out, b_out, ln_gain, ln_bias)))
    blocks_in = inputs.astype(jnp.float32).reshape(MICRO * N_DP, SLOTS, D)
    cot_blocks = cotangent.astype(jnp.float32).reshape(MICRO * N_DP, SLOTS, D)
    length_blocks = jnp.transpose(seq_lengths, (1, 0, 2)).reshape(MICRO * N_DP, SEQS).astype(jnp.int32)
    zero_delta = jnp.zeros_like(blocks_in)
    step_fn = jax.checkpoint(pair)

    def run(weights, blocks_in, deltas):
        section_params = (tuple((a[0] for a in weights)), tuple((a[1] for a in weights)))

        def scan_body(carry, item):
            block_in, delta, lengths = item
            return (carry, step_fn(section_params, block_in, delta, lengths))
        _, outs = lax.scan(scan_body, jnp.zeros((), jnp.float32), (blocks_in, deltas, length_blocks))
        return outs
    (first, second), pull = jax.vjp(run, weights, blocks_in, zero_delta)
    grad_weights, grad_in, grad_delta = pull((jnp.zeros_like(first), cot_blocks))
    section_out = jnp.stack([first, second]).reshape(2, MICRO, N_DP * SLOTS, D).astype(jnp.bfloat16)
    input_grad = jnp.stack([grad_in, grad_delta]).reshape(2, MICRO, N_DP * SLOTS, D).astype(jnp.bfloat16)
    g_attn, g_bqv, g_proj, g_bproj, g_fc, g_bfc, g_out, g_bout, g_gain, g_bias = grad_weights
    return (section_out, input_grad, g_attn, g_bqv, g_proj, g_bproj, g_fc, g_bfc, g_out, g_bout, g_gain, g_bias)
```

```python
import functools

import jax
import jax.numpy as jnp
from jax import lax
from jax.experimental import pallas as pl
from jax.experimental.pallas import tpu as pltpu
from jax.sharding import PartitionSpec as P

HEAD_DIM = 64
SCALE = HEAD_DIM**-0.5
F32 = jnp.float32
BF16 = jnp.bfloat16


def dot(left, right, dims):
    return lax.dot_general(left, right, (dims, ((), ())), preferred_element_type=F32)


NN = ((1,), (0,))
NT = ((1,), (1,))
TN = ((0,), (0,))


def layer_norm(rows, gain, shift):
    center = jnp.mean(rows, axis=-1, keepdims=True)
    centred = rows - center
    variance = jnp.mean(centred * centred, axis=-1, keepdims=True)
    return centred * lax.rsqrt(variance + 1e-05) * gain + shift


def gelu_tanh(values):
    return jax.nn.gelu(values, approximate=True)


def fill_mask(seg_col, seg_row, mask):
    total = mask.shape[0]
    query = lax.broadcasted_iota(jnp.int32, (total, total), 0)
    key = lax.broadcasted_iota(jnp.int32, (total, total), 1)
    allowed = (seg_col[...] == seg_row[...]) & (key <= query)
    mask[...] = jnp.where(allowed, 0.0, -1e30)


def bands(total):
    span = total // 2 if total % 256 == 0 else total
    return [(start, span, start + span) for start in range(0, total, span)]


def attend_kernel(heads, mixed, seg_col, seg_row, context, mask):
    fill_mask(seg_col, seg_row, mask)
    width = heads * HEAD_DIM
    total = mixed.shape[0]
    every = mixed[...]
    parts = []
    for head in range(heads):
        at = head * HEAD_DIM
        queries = every[:, at : at + HEAD_DIM] * SCALE
        keys = every[:, width + at : width + at + HEAD_DIM]
        values = every[:, 2 * width + at : 2 * width + at + HEAD_DIM]
        rows = []
        for start, span, seen in bands(total):
            scores = dot(queries[start : start + span], keys[:seen], NT)
            scores = scores + mask[start : start + span, :seen]
            expo = jnp.exp(scores - jnp.max(scores, axis=-1, keepdims=True))
            weights = expo / jnp.sum(expo, axis=-1, keepdims=True)
            rows.append(dot(weights.astype(BF16), values[:seen], NN))
        parts.append(jnp.concatenate(rows, axis=0))
    context[...] = jnp.concatenate(parts, axis=1).astype(BF16)


def attend_grad_kernel(heads, mixed, grad_context, seg_col, seg_row, grad_mixed, mask):
    fill_mask(seg_col, seg_row, mask)
    width = heads * HEAD_DIM
    total = mixed.shape[0]
    every = mixed[...]
    grads = grad_context[...]
    all_q, all_k, all_v = [], [], []
    for head in range(heads):
        at = head * HEAD_DIM
        queries = every[:, at : at + HEAD_DIM] * SCALE
        keys = every[:, width + at : width + at + HEAD_DIM]
        values = every[:, 2 * width + at : 2 * width + at + HEAD_DIM]
        grad = grads[:, at : at + HEAD_DIM]
        grad_q, grad_k, grad_v = [], [], []
        for start, span, seen in bands(total):
            here = queries[start : start + span]
            grad_here = grad[start : start + span]
            scores = dot(here, keys[:seen], NT) + mask[start : start + span, :seen]
            expo = jnp.exp(scores - jnp.max(scores, axis=-1, keepdims=True))
            probs = expo / jnp.sum(expo, axis=-1, keepdims=True)
            grad_v.append(dot(probs.astype(BF16), grad_here, TN))
            grad_probs = dot(grad_here, values[:seen], NT)
            weighted = jnp.sum(probs * grad_probs, axis=-1, keepdims=True)
            grad_scores = (probs * (grad_probs - weighted)).astype(BF16)
            grad_q.append(dot(grad_scores, keys[:seen], NN) * SCALE)
            grad_k.append(dot(grad_scores, here, TN))
        for pieces, whole in ((grad_k, all_k), (grad_v, all_v)):
            summed = pieces[-1]
            for piece in pieces[:-1]:
                rest = summed.shape[0] - piece.shape[0]
                summed = jnp.concatenate(
                    [summed[: piece.shape[0]] + piece, summed[piece.shape[0] :]], axis=0
                ) if rest else summed + piece
            whole.append(summed)
        all_q.append(jnp.concatenate(grad_q, axis=0))
    grad_mixed[...] = jnp.concatenate(all_q + all_k + all_v, axis=1).astype(BF16)


def attend(mixed, segment):
    total, width = mixed.shape
    width //= 3
    heads = width // HEAD_DIM
    return pl.pallas_call(
        functools.partial(attend_kernel, heads),
        out_shape=jax.ShapeDtypeStruct((total, width), BF16),
        scratch_shapes=[pltpu.VMEM((total, total), F32)],
        compiler_params=pltpu.CompilerParams(vmem_limit_bytes=32 * 2**20),
        cost_estimate=pl.CostEstimate(
            flops=3 * total * total * width, bytes_accessed=8 * total * width, transcendentals=heads * total * total
        ),
        name="attend",
    )(mixed, segment[:, None], segment[None, :])


def attend_grad(mixed, grad_context, segment):
    total, width = grad_context.shape
    heads = width // HEAD_DIM
    return pl.pallas_call(
        functools.partial(attend_grad_kernel, heads),
        out_shape=jax.ShapeDtypeStruct(mixed.shape, BF16),
        scratch_shapes=[pltpu.VMEM((total, total), F32)],
        compiler_params=pltpu.CompilerParams(vmem_limit_bytes=32 * 2**20),
        cost_estimate=pl.CostEstimate(
            flops=8 * total * total * width, bytes_accessed=14 * total * width, transcendentals=heads * total * total
        ),
        name="attend_grad",
    )(mixed, grad_context, segment[:, None], segment[None, :])


def partner(values, distance):
    return lax.ppermute(values, "tensor", [(i, i ^ distance) for i in range(4)])


def gather_four(own):
    far = partner(own, 2)
    return [own, partner(own, 1), far, partner(far, 1)]


def straight(pieces, index):
    odd = (index & 1) == 1
    upper = (index & 2) == 2
    low = [jnp.where(odd, pieces[k ^ 1], pieces[k]) for k in range(4)]
    return [jnp.where(upper, low[k ^ 2], low[k]) for k in range(4)]


def rows_to_batches(blocks, index):
    pieces = [lax.dynamic_index_in_dim(blocks, index ^ k, 0, keepdims=False) for k in range(4)]
    pieces = [pieces[0]] + [partner(pieces[k], k) for k in range(1, 4)]
    return jnp.concatenate(straight(pieces, index), axis=0)


def batches_to_rows(rows, index):
    own = rows.shape[0] // 4
    pieces = [lax.dynamic_slice_in_dim(rows, (index ^ k) * own, own, 0) for k in range(4)]
    pieces = [pieces[0]] + [partner(pieces[k], k) for k in range(1, 4)]
    return jnp.stack(straight(pieces, index))


def scatter_dp(values):
    count = lax.axis_size("dp")
    if count > 8:
        return lax.psum_scatter(values.astype(BF16), "dp", scatter_dimension=0, tiled=True).astype(F32)
    share = values.shape[0] // count
    me = lax.axis_index("dp")
    total = lax.dynamic_slice_in_dim(values, me * share, share, 0)
    values = values.astype(BF16)
    for step in range(1, count):
        piece = lax.dynamic_slice_in_dim(values, lax.rem(me + step, count) * share, share, 0)
        route = [(i, (i + step) % count) for i in range(count)]
        total = total + lax.ppermute(piece, "dp", route).astype(F32)
    return total


def reduce_unit(grads):
    near = partner(grads[1].astype(BF16), 1)
    cross = partner(grads[3].astype(BF16), 1)
    send = (grads[2] + cross.astype(F32)).astype(BF16)
    own = grads[0] + near.astype(F32)
    return scatter_dp(own + partner(send, 2).astype(F32))


def forward(params, rows, segment, live):
    units, biases, b_proj, b_out, ln_gain, ln_bias = params
    attn, fc, out = units
    b_q, b_v, b_fc = biases
    width = b_q[0].shape[0]
    normed = layer_norm(rows, ln_gain[0], ln_bias[0]).astype(BF16)
    middle = rows + b_proj
    mixed_all, context_all = [], []
    for k in range(4):
        bias_row = jnp.concatenate([b_q[k], jnp.zeros_like(b_q[k]), b_v[k]])
        mixed = (dot(normed, attn[k][:, : 3 * width], NN) + bias_row).astype(BF16)
        context = attend(mixed, segment)
        middle = middle + dot(context, attn[k][:, 3 * width :], NT)
        mixed_all.append(mixed)
        context_all.append(context)
    normed_two = layer_norm(middle, ln_gain[1], ln_bias[1]).astype(BF16)
    result = middle + b_out
    hidden_all, active_all = [], []
    for k in range(4):
        hidden = dot(normed_two, fc[k], NN) + b_fc[k]
        active = gelu_tanh(hidden).astype(BF16)
        result = result + dot(active, out[k], NN)
        hidden_all.append(hidden)
        active_all.append(active)
    result = (live * result).astype(BF16)
    return result, (rows, normed, mixed_all, context_all, middle, normed_two, hidden_all, active_all)


def backward(params, kept, grad_out, segment, live, with_weights):
    units, biases, b_proj, b_out, ln_gain, ln_bias = params
    attn, fc, out = units
    rows, normed, mixed_all, context_all, middle, normed_two, hidden_all, active_all = kept
    width = biases[0][0].shape[0]
    grad_final = live * grad_out
    grad_branch = grad_final.astype(BF16)
    grad_normed_two = None
    grad_hidden_all, big_out, big_fc, big_attn = [], [], [], []
    for k in range(4):
        grad_active = dot(grad_branch, out[k], NT)
        unused, gelu_pull = jax.vjp(gelu_tanh, hidden_all[k])
        grad_hidden = gelu_pull(grad_active)[0].astype(BF16)
        part = dot(grad_hidden, fc[k], NT)
        grad_normed_two = part if k == 0 else grad_normed_two + part
        grad_hidden_all.append(grad_hidden)
    if with_weights:
        big_out = [dot(grad_branch, active_all[k], TN) for k in range(4)]
        big_fc = [dot(normed_two, grad_hidden_all[k], TN) for k in range(4)]
    unused, norm_pull = jax.vjp(layer_norm, middle, ln_gain[1], ln_bias[1])
    grad_middle, g_gain_two, g_shift_two = norm_pull(grad_normed_two)
    grad_middle = grad_middle + grad_final
    grad_attn = grad_middle.astype(BF16)
    grad_normed = None
    grad_mixed_all = []
    for k in range(4):
        grad_context = dot(grad_attn, attn[k][:, 3 * width :], NN).astype(BF16)
        grad_mixed = attend_grad(mixed_all[k], grad_context, segment)
        part = dot(grad_mixed, attn[k][:, : 3 * width], NT)
        grad_normed = part if k == 0 else grad_normed + part
        grad_mixed_all.append(grad_mixed)
    unused, first_pull = jax.vjp(layer_norm, rows, ln_gain[0], ln_bias[0])
    grad_rows, g_gain_one, g_shift_one = first_pull(grad_normed)
    grad_rows = (grad_rows + grad_middle).astype(BF16)
    if not with_weights:
        return grad_rows
    big_attn = [
        jnp.concatenate(
            [dot(normed, grad_mixed_all[k], TN), dot(grad_attn, context_all[k], TN)], axis=1
        )
        for k in range(4)
    ]
    split = [
        jnp.concatenate(
            [
                jnp.sum(grad_mixed_all[k][:, :width].astype(F32), axis=0),
                jnp.sum(grad_mixed_all[k][:, 2 * width :].astype(F32), axis=0),
                jnp.sum(grad_hidden_all[k].astype(F32), axis=0),
            ]
        )
        for k in range(4)
    ]
    small = jnp.concatenate(
        [
            g_gain_one,
            g_gain_two,
            g_shift_one,
            g_shift_two,
            jnp.sum(grad_attn.astype(F32), axis=0),
            jnp.sum(grad_branch.astype(F32), axis=0),
        ]
    )
    return grad_rows, (big_attn, big_fc, big_out), split, small


def body(
    inputs,
    cotangent,
    seq_lengths,
    w_attn,
    b_qv,
    w_proj,
    b_proj,
    w_fc,
    b_fc,
    w_out,
    b_out,
    ln_gain,
    ln_bias,
):
    micro, own, model = inputs.shape
    total = own * lax.axis_size("tensor")
    width = w_attn.shape[-1]
    me = lax.axis_index("tensor")
    first = lax.axis_index("section") == 0

    unit_attn = jnp.concatenate([w_attn[0].reshape(model, 3 * width), w_proj[0].T], axis=1)
    units = (gather_four(unit_attn), gather_four(w_fc[0]), gather_four(w_out[0]))
    split_own = jnp.concatenate([b_qv[0, 0], b_qv[0, 1], b_fc[0]])
    split_all = [v.astype(F32) for v in gather_four(split_own)]
    biases = (
        [v[:width] for v in split_all],
        [v[width : 2 * width] for v in split_all],
        [v[2 * width :] for v in split_all],
    )
    params = (
        units,
        biases,
        b_proj[0].astype(F32),
        b_out[0].astype(F32),
        ln_gain[0].astype(F32),
        ln_bias[0].astype(F32),
    )

    lengths = lax.dynamic_index_in_dim(seq_lengths[0], me, 0, keepdims=False)
    ends = jnp.cumsum(lengths)
    position = jnp.arange(total, dtype=jnp.int32)
    segment = jnp.sum((position[:, None] >= ends[None, :]).astype(jnp.int32), axis=1)
    live = (position < ends[-1]).astype(F32)[:, None]

    staged = rows_to_batches(jnp.where(first, inputs, cotangent), me)
    result, unused = forward(params, staged.astype(F32), segment, live)
    received = lax.ppermute(result, "section", [(0, 1)])
    rows = jnp.where(first, staged, received).astype(F32)
    result, kept = forward(params, rows, segment, live)
    section_out = batches_to_rows(result, me)
    sent = backward(params, kept, staged.astype(F32), segment, live, False)
    coming = lax.ppermute(sent, "section", [(1, 0)])
    grad_out = jnp.where(first, coming, staged).astype(F32)
    grad_rows, big, split, small = backward(params, kept, grad_out, segment, live, True)
    input_grad = batches_to_rows(grad_rows, me)

    g_attn, g_fc, g_out = [reduce_unit(grads) for grads in big]
    g_wattn = g_attn[:, : 3 * width].reshape(-1, 3, width)
    g_wproj = g_attn[:, 3 * width :].T
    g_wout = g_out.T

    flat = lax.psum(jnp.concatenate(straight(split, me) + [small]), ("dp", "tensor"))
    piece = split[0].shape[0]
    mine = lax.dynamic_slice_in_dim(flat, me * piece, piece, 0)
    g_bqv = mine[: 2 * width].reshape(2, width)
    g_bfc = mine[2 * width :]
    sums = flat[4 * piece :].reshape(6, model)
    share = model // (lax.axis_size("dp") * lax.axis_size("tensor"))
    place = (lax.axis_index("dp") * lax.axis_size("tensor") + me) * share
    sums = lax.dynamic_slice_in_dim(sums, place, share, 1)
    return (
        section_out[None],
        input_grad[None],
        g_wattn[None],
        g_bqv[None],
        g_wproj[None],
        sums[4][None],
        g_fc[None],
        g_bfc[None],
        g_wout[None],
        sums[5][None],
        sums[0:2][None],
        sums[2:4][None],
    )


def solution(mesh):
    in_specs = (
        P(None, ("dp", "tensor"), None),
        P(None, ("dp", "tensor"), None),
        P("dp", None, None),
        P("section", None, None, "tensor"),
        P("section", None, "tensor"),
        P("section", "tensor", None),
        P("section", None),
        P("section", None, "tensor"),
        P("section", "tensor"),
        P("section", "tensor", None),
        P("section", None),
        P("section", None, None),
        P("section", None, None),
    )
    out_specs = (
        P("section", None, ("dp", "tensor"), None),
        P("section", None, ("dp", "tensor"), None),
        P("section", "dp", None, "tensor"),
        P("section", None, "tensor"),
        P("section", "tensor", "dp"),
        P("section", ("dp", "tensor")),
        P("section", "dp", "tensor"),
        P("section", "tensor"),
        P("section", "tensor", "dp"),
        P("section", ("dp", "tensor")),
        P("section", None, ("dp", "tensor")),
        P("section", None, ("dp", "tensor")),
    )
    return jax.shard_map(body, mesh=mesh, in_specs=in_specs, out_specs=out_specs, check_vma=False)
```

```python
import functools

import jax
import jax.numpy as jnp
from jax import lax
from jax.experimental import pallas as pl
from jax.experimental.pallas import tpu as pltpu
from jax.sharding import PartitionSpec as P

HEAD_DIM = 64
SCALE = HEAD_DIM**-0.5
F32 = jnp.float32
BF16 = jnp.bfloat16
PLACES = (0, 2, 1, 3)
GELU_A = (2.0 / jnp.pi) ** 0.5
GELU_B = 0.044715
VMEM_BYTES = 24 * 2**20
LONG = 2 * 10**8


def dot(left, right, dims):
    return lax.dot_general(left, right, (dims, ((), ())), preferred_element_type=F32)


NN = ((1,), (0,))
NT = ((1,), (1,))
TN = ((0,), (0,))


def normalized(rows):
    center = jnp.mean(rows, axis=-1, keepdims=True)
    centred = rows - center
    spread = lax.rsqrt(jnp.mean(centred * centred, axis=-1, keepdims=True) + 1e-05)
    return centred * spread, spread


def norm_back(rows, gain, grad):
    unit, spread = normalized(rows)
    scaled = grad * gain
    inner = jnp.mean(scaled * unit, axis=-1, keepdims=True)
    back = spread * (scaled - jnp.mean(scaled, axis=-1, keepdims=True) - unit * inner)
    return back, col_sum(grad * unit), col_sum(grad)


def col_sum(values):
    return jnp.sum(values, axis=0, keepdims=True)


def fill_mask(seg_col, seg_row, mask):
    total = mask.shape[0]
    key = lax.broadcasted_iota(jnp.int32, (total, total), 0)
    query = lax.broadcasted_iota(jnp.int32, (total, total), 1)
    allowed = (seg_col[...] == seg_row[...]) & (key <= query)
    mask[...] = jnp.where(allowed, 0.0, -1e30)


def bands(total):
    span = total // 2 if total % 256 == 0 else total
    return [(start, start + span) for start in range(0, total, span)]


def share_out(step, values, near, far):
    if near is not None:

        @pl.when(step < 2)
        def keep_near():
            near[0] = values

    for index, ref in enumerate(far):

        @pl.when(step == 2 + index)
        def keep_far(ref=ref):
            ref[...] = values


def attend_kernel(fresh, rows, seg_col, seg_row, weight, bias, *rest):
    if fresh:
        gain, shift, b_proj, total_out, normed_out, mixed_out, context_out, logsum_out, mask, total = rest
        normed = normed_out
    else:
        normed, total_out, mixed_out, context_out, logsum_out, mask, total = rest
    step = pl.program_id(0)
    width = context_out.shape[-1]
    count = rows.shape[0]

    @pl.when(step == 0)
    def start():
        fill_mask(seg_col, seg_row, mask)
        here = rows[...].astype(F32)
        if fresh:
            unit, unused = normalized(here)
            normed_out[...] = (unit * gain[...] + shift[...]).astype(BF16)
            total[...] = here + b_proj[...]
        else:
            total[...] = here

    wide = weight[0]
    mixed = (dot(normed[...], wide[:, : 3 * width], NN) + bias[0]).astype(BF16)
    mixed_out[0] = mixed
    pieces, stats = [], []
    for head in range(width // HEAD_DIM):
        at = head * HEAD_DIM
        queries = mixed[:, at : at + HEAD_DIM] * SCALE
        keys = mixed[:, width + at : width + at + HEAD_DIM]
        values = mixed[:, 2 * width + at : 2 * width + at + HEAD_DIM]
        made, logs = [], []
        for low, high in bands(count):
            scores = dot(keys[:high], queries[low:high], NT) + mask[:high, low:high]
            top = jnp.max(scores, axis=0, keepdims=True)
            expo = jnp.exp(scores - top)
            norm = jnp.sum(expo, axis=0, keepdims=True)
            made.append(dot(values[:high], expo.astype(BF16), TN) * (1.0 / norm))
            logs.append(top + jnp.log(norm))
        pieces.append(jnp.concatenate(made, axis=1))
        stats.append(jnp.concatenate(logs, axis=1))
    context = jnp.concatenate(pieces, axis=0).T.astype(BF16)
    context_out[0] = context
    stats.append(jnp.zeros((8 - len(stats), count), F32))
    logsum_out[0] = jnp.concatenate(stats, axis=0)
    total[...] += dot(context, wide[:, 3 * width :], NT)

    @pl.when(step == pl.num_programs(0) - 1)
    def finish():
        total_out[...] = total[...]


def feed_kernel(fresh, last, keep, rows, fc, out, b_fc, *rest):
    rest = list(rest)
    if fresh:
        gain, shift = rest[:2]
        rest = rest[2:]
    else:
        normed = rest.pop(0)
    if last:
        live, b_out = rest[:2]
        rest = rest[2:]
    result = rest.pop(0)
    if fresh:
        normed = rest.pop(0)
    if keep:
        slope_out, active_near, active_far = rest[0], rest[1], rest[2:4]
    total = rest[-1]
    step = pl.program_id(0)
    count = rows.shape[0]

    @pl.when(step == 0)
    def start():
        if fresh:
            unit, unused = normalized(rows[...])
            normed[...] = (unit * gain[...] + shift[...]).astype(BF16)
        total[...] = rows[...]

    made = []
    for low, high in bands(count):
        hidden = dot(normed[low:high, :], fc[0], NN) + b_fc[0]
        square = hidden * hidden
        tanh = jnp.tanh(GELU_A * hidden * (1.0 + GELU_B * square))
        upper = 0.5 * (1.0 + tanh)
        active = (hidden * upper).astype(BF16)
        total[low:high, :] += dot(active, out[0], NN)
        if keep:
            inner = GELU_A * hidden * (1.0 + 3.0 * GELU_B * square)
            slope_out[0, low:high, :] = (upper + upper * (1.0 - tanh) * inner).astype(BF16)
            made.append(active)
    if keep:
        share_out(step, jnp.concatenate(made, axis=0), active_near, active_far)

    @pl.when(step == pl.num_programs(0) - 1)
    def finish():
        if last:
            result[...] = (live[...] * (total[...] + b_out[...])).astype(BF16)
        else:
            result[...] = total[...]


def feed_back_kernel(
    grad, live, middle, slope, fc, out, gain, grad_middle, grad_attn, branch_out, near, far_one, far_two,
    b_fc_out, small, total,
):
    step = pl.program_id(0)
    count = grad.shape[0]

    @pl.when(step == 0)
    def start():
        branch_out[...] = (live[...] * grad[...].astype(F32)).astype(BF16)
        total[...] = jnp.zeros_like(total)

    bias_sum = 0.0
    made = []
    for low, high in bands(count):
        grad_active = dot(branch_out[low:high, :], out[0], NT)
        grad_hidden = (grad_active * slope[0, low:high, :].astype(F32)).astype(BF16)
        bias_sum = bias_sum + col_sum(grad_hidden.astype(F32))
        total[low:high, :] += dot(grad_hidden, fc[0], NT)
        made.append(grad_hidden)
    b_fc_out[0] = bias_sum
    share_out(step, jnp.concatenate(made, axis=0), near, (far_one, far_two))

    @pl.when(step == pl.num_programs(0) - 1)
    def finish():
        back, gain_sum, shift_sum = norm_back(middle[...], gain[...], total[...])
        back = back + live[...] * grad[...].astype(F32)
        grad_middle[...] = back
        rounded = back.astype(BF16)
        grad_attn[...] = rounded
        sums = [gain_sum, shift_sum, col_sum(rounded.astype(F32)), col_sum(branch_out[...].astype(F32))]
        small[...] = jnp.concatenate(sums + [jnp.zeros((4, gain_sum.shape[1]), F32)], axis=0)


def attend_back_kernel(
    grad_attn, grad_middle, rows, seg_col, seg_row, weight, mixed, context, logsum, gain,
    grad_rows, near, far_one, far_two, bias_out, small, mask, total,
):
    step = pl.program_id(0)
    width = context.shape[-1]
    count = grad_attn.shape[0]

    @pl.when(step == 0)
    def start():
        fill_mask(seg_col, seg_row, mask)
        total[...] = jnp.zeros_like(total)

    wide = weight[0]
    grad_context = dot(grad_attn[...], wide[:, 3 * width :], NN).astype(BF16)
    product = (grad_context.astype(F32) * context[0].astype(F32)).T
    every = mixed[0]
    all_q, all_k, all_v = [], [], []
    for head in range(width // HEAD_DIM):
        at = head * HEAD_DIM
        queries = every[:, at : at + HEAD_DIM] * SCALE
        keys = every[:, width + at : width + at + HEAD_DIM]
        values = every[:, 2 * width + at : 2 * width + at + HEAD_DIM]
        grad = grad_context[:, at : at + HEAD_DIM]
        weighted = col_sum(product[at : at + HEAD_DIM, :])
        grad_q, grad_k, grad_v = [], [], []
        for low, high in bands(count):
            scores = dot(keys[:high], queries[low:high], NT) + mask[:high, low:high]
            probs = jnp.exp(scores - logsum[0, head : head + 1, low:high])
            grad_probs = dot(values[:high], grad[low:high], NT)
            grad_scores = (probs * (grad_probs - weighted[:, low:high])).astype(BF16)
            grad_v.append(dot(probs.astype(BF16), grad[low:high], NN))
            grad_k.append(dot(grad_scores, queries[low:high], NN))
            grad_q.append(dot(keys[:high], grad_scores, TN) * SCALE)
        for parts, whole in ((grad_k, all_k), (grad_v, all_v)):
            summed = parts[-1]
            for part in parts[:-1]:
                reach = part.shape[0]
                summed = jnp.concatenate([summed[:reach] + part, summed[reach:]], axis=0)
            whole.append(summed)
        all_q.append(jnp.concatenate(grad_q, axis=1))
    first = jnp.concatenate(all_q, axis=0).T
    grad_mixed = jnp.concatenate([first] + all_k + all_v, axis=1).astype(BF16)

    share_out(step, grad_mixed, near, ())
    both = jnp.concatenate([grad_mixed, context[0]], axis=1)
    share_out(step, both, None, (far_one, far_two))
    sums = col_sum(grad_mixed.astype(F32))
    spare = jnp.zeros((1, bias_out.shape[-1] - 2 * width), F32)
    bias_out[0] = jnp.concatenate([sums[:, :width], sums[:, 2 * width :], spare], axis=1)
    total[...] += dot(grad_mixed, wide[:, : 3 * width], NT)

    @pl.when(step == pl.num_programs(0) - 1)
    def finish():
        back, gain_sum, shift_sum = norm_back(rows[...].astype(F32), gain[...], total[...])
        grad_rows[...] = (grad_middle[...] + back).astype(BF16)
        small[...] = jnp.concatenate([gain_sum, shift_sum, jnp.zeros((6, gain_sum.shape[1]), F32)], axis=0)


def outer_kernel(pairs, chunks, *refs):
    outs = refs[5 * pairs :]
    for place in range(2):
        sums, taken = [], 0
        for index in range(pairs):
            left, left_other, right, *others = refs[5 * index : 5 * index + 5]
            columns = right.shape[-1]
            away = others[place][...][:, taken : taken + columns] if pairs > 1 else others[place][...]
            taken += columns
            sums.append(dot(left[...], right[place], TN) + dot(left_other[...], away, TN))
        whole = sums[0] if pairs == 1 else jnp.concatenate(sums, axis=1)
        columns = whole.shape[1] // chunks
        for index in range(chunks):
            part = whole[:, index * columns : (index + 1) * columns]
            outs[2 * index + place][...] = part.astype(BF16) if place else part


def combine_kernel(bit, keep, keep_other, arrived, arrived_other, kept, sent):
    kept[0] = keep[0, 0] + arrived[0, 0].astype(F32)
    sent[0] = (keep_other[0, 0] + arrived_other[0, 0].astype(F32)).astype(sent.dtype)


def block(shape):
    return pl.BlockSpec(shape, lambda step: (0,) * len(shape))


def stepped(shape):
    return pl.BlockSpec((1,) + shape[1:], lambda step: (step,) + (0,) * (len(shape) - 1))


def near_spec(shape):
    return pl.BlockSpec((1,) + shape[1:], lambda step: (jnp.minimum(step, 1), 0, 0))


def call(kernel, name, steps, ins, outs, scratch, waits=(), cost=1):
    count = len(ins)
    skip = count + len(waits)

    def run(*refs):
        kernel(*refs[:count], *refs[skip:])

    return pl.pallas_call(
        run,
        grid=(steps,),
        in_specs=[kind(value.shape) for value, kind in ins] + [pl.BlockSpec(memory_space=pl.ANY)] * len(waits),
        out_specs=[kind(shape) for shape, dtype, kind in outs],
        out_shape=[jax.ShapeDtypeStruct(shape, dtype) for shape, dtype, kind in outs],
        scratch_shapes=scratch,
        compiler_params=pltpu.CompilerParams(vmem_limit_bytes=VMEM_BYTES),
        cost_estimate=pl.CostEstimate(flops=1, bytes_accessed=cost, transcendentals=0),
        name=name,
    )(*[value for value, kind in ins], *waits)


def attend(rows, segment, weight, bias, normed=None, first=None, waits=(), cost=1):
    steps = weight.shape[0]
    total, model = rows.shape
    width = bias.shape[-1] // 3
    ins = [(rows, block), (segment[:, None], block), (segment[None, :], block), (weight, stepped), (bias, stepped)]
    outs = [((total, model), F32, block)]
    if first is None:
        ins.append((normed, block))
    else:
        ins += [(v, block) for v in first]
        outs.append(((total, model), BF16, block))
    outs += [
        ((steps, total, 3 * width), BF16, stepped),
        ((steps, total, width), BF16, stepped),
        ((steps, 8, total), F32, stepped),
    ]
    return call(
        functools.partial(attend_kernel, first is not None), "attend", steps, ins, outs,
        [pltpu.VMEM((total, total), F32), pltpu.VMEM((total, model), F32)], waits, cost,
    )


def feed(rows, fc, out, b_fc, normed=None, first=None, last=None, keep=False, cost=1):
    steps = fc.shape[0]
    total, model = rows.shape
    units = fc.shape[-1]
    ins = [(rows, block), (fc, stepped), (out, stepped), (b_fc, stepped)]
    outs = [((total, model), F32 if last is None else BF16, block)]
    if first is None:
        ins.append((normed, block))
    else:
        ins += [(v, block) for v in first]
        outs.append(((total, model), BF16, block))
    if last is not None:
        ins += [(v, block) for v in last]
    if keep:
        outs += [
            ((steps, total, units), BF16, stepped),
            ((steps // 2, total, units), BF16, near_spec),
            ((total, units), BF16, block),
            ((total, units), BF16, block),
        ]
    return call(
        functools.partial(feed_kernel, first is not None, last is not None, keep), "feed", steps, ins, outs,
        [pltpu.VMEM((total, model), F32)], (), cost,
    )


def feed_back(grad, live, middle, slope, fc, out, gain, waits=(), cost=1):
    steps = fc.shape[0]
    total, model = grad.shape
    units = fc.shape[-1]
    ins = [(grad, block), (live, block), (middle, block), (slope, stepped), (fc, stepped), (out, stepped), (gain, block)]
    outs = [
        ((total, model), F32, block),
        ((total, model), BF16, block),
        ((total, model), BF16, block),
        ((steps // 2, total, units), BF16, near_spec),
        ((total, units), BF16, block),
        ((total, units), BF16, block),
        ((steps, 1, units), F32, stepped),
        ((8, model), F32, block),
    ]
    return call(
        feed_back_kernel, "feed_back", steps, ins, outs, [pltpu.VMEM((total, model), F32)], waits, cost
    )


def attend_back(grad_attn, grad_middle, rows, segment, weight, mixed, context, logsum, gain, waits=(), cost=1):
    steps = weight.shape[0]
    total, model = grad_attn.shape
    width = context.shape[-1]
    ins = [
        (grad_attn, block), (grad_middle, block), (rows, block), (segment[:, None], block), (segment[None, :], block),
        (weight, stepped), (mixed, stepped), (context, stepped), (logsum, stepped), (gain, block),
    ]
    outs = [
        ((total, model), BF16, block),
        ((steps // 2, total, 3 * width), BF16, near_spec),
        ((total, 4 * width), BF16, block),
        ((total, 4 * width), BF16, block),
        ((steps, 1, model), F32, stepped),
        ((8, model), F32, block),
    ]
    return call(
        attend_back_kernel, "attend_back", steps, ins, outs,
        [pltpu.VMEM((total, total), F32), pltpu.VMEM((total, model), F32)], waits, cost,
    )


def outer(*pairs, chunks=1, waits=()):
    ins, columns = [], 0
    for left, left_other, right, others in pairs:
        ins += [(left, block), (left_other, block), (right, block)] + [(v, block) for v in others]
        columns += right.shape[-1]
    model = pairs[0][0].shape[1]
    outs = [((model, columns // chunks), F32, block), ((model, columns // chunks), BF16, block)] * chunks
    made = call(functools.partial(outer_kernel, len(pairs), chunks), "outer", 1, ins, outs, [], waits)
    return [list(made[2 * index : 2 * index + 2]) for index in range(chunks)]


def combine(keep, arrived, bit, kind, waits=()):
    pairs, unused, rows, columns = keep.shape

    def run(*refs):
        combine_kernel(*refs[:5], *refs[5 + len(waits) :])

    def spec(flip):
        return pl.BlockSpec((1, 1, rows, columns), lambda step, where: (step, flip + (1 - 2 * flip) * where[0], 0, 0))

    ends = pl.BlockSpec((1, rows, columns), lambda step, where: (step, 0, 0))
    return pl.pallas_call(
        run,
        grid_spec=pltpu.PrefetchScalarGridSpec(
            num_scalar_prefetch=1,
            grid=(pairs,),
            in_specs=[spec(0), spec(1), spec(0), spec(1)] + [pl.BlockSpec(memory_space=pl.ANY)] * len(waits),
            out_specs=[ends, ends],
        ),
        out_shape=[
            jax.ShapeDtypeStruct((pairs, rows, columns), F32),
            jax.ShapeDtypeStruct((pairs, rows, columns), kind),
        ],
        compiler_params=pltpu.CompilerParams(vmem_limit_bytes=VMEM_BYTES),
        cost_estimate=pl.CostEstimate(flops=1, bytes_accessed=1, transcendentals=0),
        name="combine",
    )(bit, keep, keep, arrived, arrived, *waits)


def partner(values, distance):
    return lax.ppermute(values, "tensor", [(i, i ^ distance) for i in range(4)])


def together(*values):
    return lax.optimization_barrier(values)


def dp_paired():
    return lax.axis_size("dp") % 2 == 0


def half_of(own, shared):
    odd = lax.axis_index("dp") & 1
    return lax.dynamic_slice_in_dim(own, odd * (shared // 2), shared // 2, 0)


def swapped(mine, rest):
    odd = (lax.axis_index("dp") & 1) == 1
    other = lax.ppermute(mine, "dp", [(i, i ^ 1) for i in range(lax.axis_size("dp"))])
    return jnp.concatenate([jnp.where(odd, other, mine), jnp.where(odd, mine, other)] + rest, axis=0)


def straight(pieces, index):
    odd = (index & 1) == 1
    upper = (index & 2) == 2
    low = [jnp.where(odd, pieces[k ^ 1], pieces[k]) for k in range(4)]
    return [jnp.where(upper, low[k ^ 2], low[k]) for k in range(4)]


def rows_to_batches(first, inputs, cotangent, index):
    pieces = []
    for k in range(4):
        both = [lax.dynamic_index_in_dim(v, index ^ k, 0, keepdims=False) for v in (inputs, cotangent)]
        pieces.append(jnp.where(first, both[0], both[1]))
    pieces = [pieces[0]] + [partner(pieces[k], k) for k in range(1, 4)]
    return jnp.concatenate(straight(pieces, index), axis=0)


def batches_to_rows(rows, index):
    own = rows.shape[0] // 4
    pieces = [lax.dynamic_slice_in_dim(rows, (index ^ k) * own, own, 0) for k in range(4)]
    pieces = [pieces[0]] + [partner(pieces[k], k) for k in range(1, 4)]
    return jnp.stack(straight(pieces, index))


def dp_stages():
    count = lax.axis_size("dp")
    return [1 << i for i in range(count.bit_length() - 1)] if count & (count - 1) == 0 else None


class Reduction:
    def __init__(self, keep, arriving, kind):
        self.keep, self.arriving, self.kind = keep, arriving, kind
        self.share = keep.shape[0] // lax.axis_size("dp")
        self.left = dp_stages()

    def begin(self, *waits):
        distance = self.left.pop(0)
        columns = self.keep.shape[-1]
        bit = (lax.axis_index("dp") // distance) & 1
        shape = (self.keep.size // (2 * columns * self.share), 2, self.share, columns)
        self.keep, sent = combine(
            self.keep.reshape(shape), self.arriving.reshape(shape), bit[None], self.kind, waits
        )
        total = lax.axis_size("dp")
        self.arriving = lax.ppermute(sent, "dp", [(i, i ^ distance) for i in range(total)])
        return sent

    def result(self, *waits):
        if self.left is None:
            whole = (self.keep + self.arriving.astype(F32)).astype(self.kind)
            return lax.psum_scatter(whole, "dp", scatter_dimension=0, tiled=True).astype(F32)
        while self.left:
            self.begin(*waits)
        whole = self.keep + self.arriving.astype(F32)
        return whole.reshape(whole.shape[-2:])


def reduce_small(sums, split):
    come = partner(jnp.concatenate([sums, split[1], split[3]]), 1)
    whole = jnp.concatenate([sums, split[0]]) + come[:8]
    whole = whole + partner(jnp.concatenate([whole[:6], split[2] + come[8:]]), 2)
    stages = dp_stages()
    if stages is None:
        return lax.psum(whole, "dp")
    count = lax.axis_size("dp")
    for distance in stages:
        whole = whole + lax.ppermute(whole, "dp", [(i, i ^ distance) for i in range(count)])
    return whole


def body(
    inputs,
    cotangent,
    seq_lengths,
    w_attn,
    b_qv,
    w_proj,
    b_proj,
    w_fc,
    b_fc,
    w_out,
    b_out,
    ln_gain,
    ln_bias,
):
    micro, own, model = inputs.shape
    total = own * lax.axis_size("tensor")
    width = w_attn.shape[-1]
    groups = lax.axis_size("dp")
    me = lax.axis_index("tensor")
    first = lax.axis_index("section") == 0

    units = w_fc.shape[-1]
    shared = units // 3 * 2 if units % 48 == 0 else units
    unit_attn = jnp.concatenate([w_attn[0].reshape(model, 3 * width), w_proj[0].T], axis=1)
    paired = dp_paired()
    first_sent = half_of(unit_attn, model) if paired else unit_attn
    first_sent, inputs, cotangent, b_fc = together(first_sent, inputs, cotangent, b_fc)
    attn_far = partner(first_sent, 2)
    staged = rows_to_batches(first, inputs, cotangent, me)
    split_own = jnp.concatenate([b_qv[0, 0], jnp.zeros_like(b_qv[0, 0]), b_qv[0, 1], b_fc[0]])
    split_far = partner(split_own, 2)
    split_all = [split_own, partner(split_own, 1), split_far, partner(split_far, 1)]
    b_mixed = [v[None, None, : 3 * width].astype(F32) for v in split_all]
    b_fcs = [v[None, None, 3 * width :].astype(F32) for v in split_all]
    b_proj = b_proj.astype(F32)
    b_out = b_out.astype(F32)
    ln_gain = ln_gain[0].astype(F32)
    ln_bias = ln_bias[0].astype(F32)
    norm_one = (ln_gain[0:1], ln_bias[0:1], b_proj)
    norm_two = (ln_gain[1:2], ln_bias[1:2])

    lengths = lax.dynamic_index_in_dim(seq_lengths[0], me, 0, keepdims=False)
    ends = jnp.cumsum(lengths)
    position = jnp.arange(total, dtype=jnp.int32)
    segment = jnp.sum((position[:, None] >= ends[None, :]).astype(jnp.int32), axis=1)
    live = (position < ends[-1]).astype(F32)[:, None]
    last = (live, b_out)

    def attend_one(middle, k, normed, cost=1):
        return attend(middle, segment, attn[k][None], b_mixed[k], normed=normed, cost=cost)[0]

    def feed_one(result, k, normed, ending=None, cost=1):
        return feed(result, fc[k][None], out[k][None], b_fcs[k], normed=normed, last=ending, cost=cost)[0]

    attn = {0: unit_attn, 1: partner(unit_attn, 1)}
    fc = {0: w_fc[0], 1: partner(w_fc[0], 1)}
    out = {0: w_out[0], 1: partner(w_out[0], 1)}
    fc_sent, staged = together(half_of(w_fc[0], model) if paired else w_fc[0], staged)
    fc_far = partner(fc_sent, 2)
    middle, normed = attend(
        staged, segment, attn[0][None], b_mixed[0], first=norm_one, waits=split_all[2:], cost=LONG
    )[:2]
    if paired:
        attn_far = swapped(attn_far, [])
        out_sent, rest, fc_far, middle = together(half_of(w_out[0], shared), w_out[0, shared:], fc_far, middle)
        fc_far = swapped(fc_far, [])
        out_far, rest = partner(out_sent, 2), [partner(rest, 2)] if shared < units else []
    else:
        out_sent, middle = together(w_out[0], middle)
        out_far = partner(out_sent, 2)
    middle = attend_one(middle, 1, normed, LONG)
    attn[2], attn[3] = attn_far, partner(attn_far, 1)
    middle = attend_one(middle, 2, normed, LONG)
    middle = attend_one(middle, 3, normed, LONG)
    result, normed = feed(middle, fc[0][None], out[0][None], b_fcs[0], first=norm_two, cost=LONG)
    if paired:
        out_far = swapped(out_far, rest)
    result = feed_one(result, 1, normed, cost=LONG)
    fc[2], fc[3] = fc_far, partner(fc_far, 1)
    out[2], out[3] = out_far, partner(out_far, 1)
    result = feed_one(result, 2, normed)
    result = feed_one(result, 3, normed, last)
    received = lax.ppermute(result, "section", [(0, 1)])

    attn, fc, out, result = together(*[[v[k] for k in PLACES] for v in (attn, fc, out)], result)
    attn, fc, out = [jnp.stack(v) for v in (attn, fc, out)]
    b_mixed, b_fcs = [jnp.concatenate([v[k] for k in PLACES]) for v in (b_mixed, b_fcs)]
    rows = jnp.where(first, staged, received)
    middle, normed, mixed, context, logsum = attend(rows, segment, attn, b_mixed, first=norm_one)
    result, normed_two, slope, active, *active_away = feed(
        middle, fc, out, b_fcs, first=norm_two, last=last, keep=True
    )
    section_out = batches_to_rows(result, me)
    normed_other = partner(normed, 1)
    normed_two_other = partner(normed_two, 1)
    active_other = [partner(v, 1) for v in active_away]

    fed = feed_back(staged, live, middle, slope, fc, out, norm_two[0])
    early = (section_out, normed_other, normed_two_other, *active_other)
    passed = attend_back(fed[1], fed[0], rows, segment, attn, mixed, context, logsum, norm_one[0], early)
    coming = lax.ppermute(passed[0], "section", [(1, 0)])
    grad_out = jnp.where(first, coming, staged)

    branch = (live * grad_out.astype(F32)).astype(BF16)
    ((keep_out, send_out),) = outer((branch, partner(branch, 1), active, active_other))
    sum_out = Reduction(keep_out, partner(send_out, 2), BF16)
    middle_grad, grad_attn, branch, hid, hid_one, hid_two, g_bfc, small_two = feed_back(
        grad_out, live, middle, slope, fc, out, norm_two[0], (send_out,), LONG
    )
    hid_other = [partner(hid_one, 1), partner(hid_two, 1)]
    ((keep_fc, send_fc),) = outer((normed_two, normed_two_other, hid, hid_other))
    sum_fc = Reduction(keep_fc, partner(send_fc, 2), BF16)
    staggered = sum_out.left is not None
    ready = [sum_out.begin(send_fc)] if staggered else []
    grad_rows, mix, mix_one, mix_two, g_mixed, small_one = attend_back(
        grad_attn, middle_grad, rows, segment, attn, mixed, context, logsum, norm_one[0], (send_fc, *ready), LONG
    )
    mix_other = [partner(mix_one, 1), partner(mix_two, 1)]
    kept = outer(
        (normed, normed_other, mix, mix_other),
        (grad_attn, partner(grad_attn, 1), context[:2], mix_other),
        chunks=2,
    )
    sums_attn = [Reduction(keep, partner(send, 2), BF16) for keep, send in kept]
    if staggered:
        sum_out.begin(kept[0][1])
        sum_fc.begin(kept[1][1])
        sums_attn[0].arriving, small_one, small_two, g_mixed, g_bfc, grad_rows = together(
            sums_attn[0].arriving, small_one, small_two, g_mixed, g_bfc, grad_rows
        )
        sums_attn[0].begin()
        sums_attn[1].begin()
    input_grad = batches_to_rows(grad_rows, me)
    g_out, g_fc = sum_out.result(), sum_fc.result()
    g_attn = jnp.concatenate([v.result() for v in sums_attn], axis=1)

    g_wattn = g_attn[:, : 3 * width].reshape(-1, 3, width)
    g_wproj = g_attn[:, 3 * width :].T
    g_wout = g_out.T

    share = model // (groups * 4)
    split = [jnp.concatenate([g_mixed[at], g_bfc[at]]) for at in (PLACES.index(k) for k in range(4))]
    sums = reduce_small(jnp.concatenate([small_one[:2], small_two[:4]]), split)
    g_bqv = sums[6, : 2 * width].reshape(2, width)
    g_bfc = sums[7]
    sums = lax.dynamic_slice_in_dim(sums, (lax.axis_index("dp") * 4 + me) * share, share, 1)
    return (
        section_out[None],
        input_grad[None],
        g_wattn[None],
        g_bqv[None],
        g_wproj[None],
        sums[4][None],
        g_fc[None],
        g_bfc[None],
        g_wout[None],
        sums[5][None],
        jnp.stack([sums[0], sums[2]])[None],
        jnp.stack([sums[1], sums[3]])[None],
    )


def solution(mesh):
    in_specs = (
        P(None, ("dp", "tensor"), None),
        P(None, ("dp", "tensor"), None),
        P("dp", None, None),
        P("section", None, None, "tensor"),
        P("section", None, "tensor"),
        P("section", "tensor", None),
        P("section", None),
        P("section", None, "tensor"),
        P("section", "tensor"),
        P("section", "tensor", None),
        P("section", None),
        P("section", None, None),
        P("section", None, None),
    )
    out_specs = (
        P("section", None, ("dp", "tensor"), None),
        P("section", None, ("dp", "tensor"), None),
        P("section", "dp", None, "tensor"),
        P("section", None, "tensor"),
        P("section", "tensor", "dp"),
        P("section", ("dp", "tensor")),
        P("section", "dp", "tensor"),
        P("section", "tensor"),
        P("section", "tensor", "dp"),
        P("section", ("dp", "tensor")),
        P("section", None, ("dp", "tensor")),
        P("section", None, ("dp", "tensor")),
    )
    return jax.shard_map(body, mesh=mesh, in_specs=in_specs, out_specs=out_specs, check_vma=False)
```

```python
import functools

import jax
import jax.numpy as jnp
from jax import lax
from jax.experimental import pallas as pl
from jax.experimental.pallas import tpu as pltpu
from jax.sharding import PartitionSpec as P

HEAD_DIM = 64
SCALE = HEAD_DIM**-0.5
F32 = jnp.float32
BF16 = jnp.bfloat16
PLACES = (0, 2, 1, 3)
GELU_A = (2.0 / jnp.pi) ** 0.5
GELU_B = 0.044715
VMEM_BYTES = 24 * 2**20
LONG = 10**10
MID = 1


def dot(left, right, dims):
    return lax.dot_general(left, right, (dims, ((), ())), preferred_element_type=F32)


NN = ((1,), (0,))
NT = ((1,), (1,))
TN = ((0,), (0,))


def normalized(rows):
    center = jnp.mean(rows, axis=-1, keepdims=True)
    centred = rows - center
    spread = lax.rsqrt(jnp.mean(centred * centred, axis=-1, keepdims=True) + 1e-05)
    return centred * spread, spread


def norm_back(rows, gain, grad):
    unit, spread = normalized(rows)
    scaled = grad * gain
    inner = jnp.mean(scaled * unit, axis=-1, keepdims=True)
    back = spread * (scaled - jnp.mean(scaled, axis=-1, keepdims=True) - unit * inner)
    return back, col_sum(grad * unit), col_sum(grad)


def col_sum(values):
    return jnp.sum(values, axis=0, keepdims=True)


def fill_mask(seg_col, seg_row, mask):
    total = mask.shape[0]
    key = lax.broadcasted_iota(jnp.int32, (total, total), 0)
    query = lax.broadcasted_iota(jnp.int32, (total, total), 1)
    allowed = (seg_col[...] == seg_row[...]) & (key <= query)
    mask[...] = jnp.where(allowed, 0.0, -1e30)


def bands(total):
    span = total // 2 if total % 256 == 0 else total
    return [(start, start + span) for start in range(0, total, span)]


def share_out(step, values, near, far):
    if near is not None:

        @pl.when(step < 2)
        def keep_near():
            near[0] = values

    for index, refs in enumerate(far):

        @pl.when(step == 2 + index)
        def keep_far(refs=refs):
            rows = values.shape[0] // len(refs)
            for part, ref in enumerate(refs):
                ref[...] = values[part * rows : (part + 1) * rows]


def attend_kernel(fresh, rows, seg_col, seg_row, weight, bias, *rest):
    if fresh:
        gain, shift, b_proj, total_out, normed_out, mixed_out, context_out, logsum_out, mask, total = rest
        normed = normed_out
    else:
        normed, total_out, mixed_out, context_out, logsum_out, mask, total = rest
    step = pl.program_id(0)
    width = context_out.shape[-1]
    count = rows.shape[0]

    @pl.when(step == 0)
    def start():
        fill_mask(seg_col, seg_row, mask)
        here = rows[...].astype(F32)
        if fresh:
            unit, unused = normalized(here)
            normed_out[...] = (unit * gain[...] + shift[...]).astype(BF16)
            total[...] = here + b_proj[...]
        else:
            total[...] = here

    wide = weight[0]
    mixed = (dot(normed[...], wide[:, : 3 * width], NN) + bias[0]).astype(BF16)
    mixed_out[0] = mixed
    pieces, stats = [], []
    for head in range(width // HEAD_DIM):
        at = head * HEAD_DIM
        queries = mixed[:, at : at + HEAD_DIM] * SCALE
        keys = mixed[:, width + at : width + at + HEAD_DIM]
        values = mixed[:, 2 * width + at : 2 * width + at + HEAD_DIM]
        made, logs = [], []
        for low, high in bands(count):
            scores = dot(keys[:high], queries[low:high], NT) + mask[:high, low:high]
            top = jnp.max(scores, axis=0, keepdims=True)
            expo = jnp.exp(scores - top)
            norm = jnp.sum(expo, axis=0, keepdims=True)
            made.append(dot(values[:high], expo.astype(BF16), TN) * (1.0 / norm))
            logs.append(top + jnp.log(norm))
        pieces.append(jnp.concatenate(made, axis=1))
        stats.append(jnp.concatenate(logs, axis=1))
    context = jnp.concatenate(pieces, axis=0).T.astype(BF16)
    context_out[0] = context
    stats.append(jnp.zeros((8 - len(stats), count), F32))
    logsum_out[0] = jnp.concatenate(stats, axis=0)
    total[...] += dot(context, wide[:, 3 * width :], NT)

    @pl.when(step == pl.num_programs(0) - 1)
    def finish():
        total_out[...] = total[...]


def feed_kernel(fresh, last, keep, rows, fc, out, b_fc, *rest):
    rest = list(rest)
    if fresh:
        gain, shift = rest[:2]
        rest = rest[2:]
    else:
        normed = rest.pop(0)
    if last:
        live, b_out = rest[:2]
        rest = rest[2:]
    result = rest.pop(0)
    if fresh:
        normed = rest.pop(0)
    if keep:
        slope_out, active_near, active_far = rest[0], rest[1], (rest[2:3], rest[3:4])
    total = rest[-1]
    step = pl.program_id(0)
    count = rows.shape[0]

    @pl.when(step == 0)
    def start():
        if fresh:
            unit, unused = normalized(rows[...])
            normed[...] = (unit * gain[...] + shift[...]).astype(BF16)
        total[...] = rows[...]

    made = []
    for low, high in bands(count):
        hidden = dot(normed[low:high, :], fc[0], NN) + b_fc[0]
        square = hidden * hidden
        tanh = jnp.tanh(GELU_A * hidden * (1.0 + GELU_B * square))
        upper = 0.5 * (1.0 + tanh)
        active = (hidden * upper).astype(BF16)
        total[low:high, :] += dot(active, out[0], NN)
        if keep:
            inner = GELU_A * hidden * (1.0 + 3.0 * GELU_B * square)
            slope_out[0, low:high, :] = (upper + upper * (1.0 - tanh) * inner).astype(BF16)
            made.append(active)
    if keep:
        share_out(step, jnp.concatenate(made, axis=0), active_near, active_far)

    @pl.when(step == pl.num_programs(0) - 1)
    def finish():
        if last:
            result[...] = (live[...] * (total[...] + b_out[...])).astype(BF16)
        else:
            result[...] = total[...]


def feed_back_kernel(
    grad, live, middle, slope, fc, out, gain, grad_middle, grad_attn, attn_high, attn_low, branch_out, near,
    far_one, far_one_low, far_two, far_two_low, b_fc_out, small, total,
):
    step = pl.program_id(0)
    count = grad.shape[0]

    @pl.when(step == 0)
    def start():
        branch_out[...] = (live[...] * grad[...].astype(F32)).astype(BF16)
        total[...] = jnp.zeros_like(total)

    bias_sum = 0.0
    made = []
    for low, high in bands(count):
        grad_active = dot(branch_out[low:high, :], out[0], NT)
        grad_hidden = (grad_active * slope[0, low:high, :].astype(F32)).astype(BF16)
        bias_sum = bias_sum + col_sum(grad_hidden.astype(F32))
        total[low:high, :] += dot(grad_hidden, fc[0], NT)
        made.append(grad_hidden)
    b_fc_out[0] = bias_sum
    share_out(step, jnp.concatenate(made, axis=0), near, ((far_one, far_one_low), (far_two, far_two_low)))

    @pl.when(step == pl.num_programs(0) - 1)
    def finish():
        back, gain_sum, shift_sum = norm_back(middle[...], gain[...], total[...])
        back = back + live[...] * grad[...].astype(F32)
        grad_middle[...] = back
        rounded = back.astype(BF16)
        grad_attn[...] = rounded
        attn_high[...] = rounded[: count // 2]
        attn_low[...] = rounded[count // 2 :]
        sums = [gain_sum, shift_sum, col_sum(rounded.astype(F32)), col_sum(branch_out[...].astype(F32))]
        small[...] = jnp.concatenate(sums + [jnp.zeros((4, gain_sum.shape[1]), F32)], axis=0)


def attend_back_kernel(
    grad_attn, grad_middle, rows, seg_col, seg_row, weight, mixed, context, logsum, gain, small_two, b_fc,
    grad_rows, near, far_one, far_one_low, far_two, far_two_low, pack, mask, total,
):
    step = pl.program_id(0)
    width = context.shape[-1]
    count = grad_attn.shape[0]

    @pl.when(step == 0)
    def start():
        fill_mask(seg_col, seg_row, mask)
        total[...] = jnp.zeros_like(total)

    wide = weight[0]
    grad_context = dot(grad_attn[...], wide[:, 3 * width :], NN).astype(BF16)
    product = (grad_context.astype(F32) * context[0].astype(F32)).T
    every = mixed[0]
    all_q, all_k, all_v = [], [], []
    for head in range(width // HEAD_DIM):
        at = head * HEAD_DIM
        queries = every[:, at : at + HEAD_DIM] * SCALE
        keys = every[:, width + at : width + at + HEAD_DIM]
        values = every[:, 2 * width + at : 2 * width + at + HEAD_DIM]
        grad = grad_context[:, at : at + HEAD_DIM]
        weighted = col_sum(product[at : at + HEAD_DIM, :])
        grad_q, grad_k, grad_v = [], [], []
        for low, high in bands(count):
            scores = dot(keys[:high], queries[low:high], NT) + mask[:high, low:high]
            probs = jnp.exp(scores - logsum[0, head : head + 1, low:high])
            grad_probs = dot(values[:high], grad[low:high], NT)
            grad_scores = (probs * (grad_probs - weighted[:, low:high])).astype(BF16)
            grad_v.append(dot(probs.astype(BF16), grad[low:high], NN))
            grad_k.append(dot(grad_scores, queries[low:high], NN))
            grad_q.append(dot(keys[:high], grad_scores, TN) * SCALE)
        for parts, whole in ((grad_k, all_k), (grad_v, all_v)):
            summed = parts[-1]
            for part in parts[:-1]:
                reach = part.shape[0]
                summed = jnp.concatenate([summed[:reach] + part, summed[reach:]], axis=0)
            whole.append(summed)
        all_q.append(jnp.concatenate(grad_q, axis=1))
    first = jnp.concatenate(all_q, axis=0).T
    grad_mixed = jnp.concatenate([first] + all_k + all_v, axis=1).astype(BF16)

    share_out(step, grad_mixed, near, ())
    both = jnp.concatenate([grad_mixed, context[0]], axis=1)
    share_out(step, both, None, ((far_one, far_one_low), (far_two, far_two_low)))
    sums = col_sum(grad_mixed.astype(F32))
    spare = jnp.zeros((1, pack.shape[-1] - 2 * width), F32)
    pack[pl.ds(8 + step, 1), :] = jnp.concatenate([sums[:, :width], sums[:, 2 * width :], spare], axis=1)
    total[...] += dot(grad_mixed, wide[:, : 3 * width], NT)

    @pl.when(step == pl.num_programs(0) - 1)
    def finish():
        back, gain_sum, shift_sum = norm_back(rows[...].astype(F32), gain[...], total[...])
        grad_rows[...] = (grad_middle[...] + back).astype(BF16)
        spare = jnp.zeros((2, gain_sum.shape[1]), F32)
        pack[:8, :] = jnp.concatenate([gain_sum, shift_sum, small_two[:4, :], spare], axis=0)
        pack[12:, :] = jnp.concatenate([b_fc[place] for place in range(4)], axis=0)


def joined(refs):
    values = [ref[...] for ref in refs]
    return jnp.concatenate(values, axis=0) if len(values) > 1 else values[0]


def outer_kernel(pairs, chunks, spans, halves, extra, *refs):
    ends = [sum(2 + span + 2 * halves for span in spans[:index]) for index in range(pairs + 1)]
    outs = refs[ends[-1] + 2 * extra :]
    for place in range(2):
        sums, taken = [], 0
        for index in range(pairs):
            left, *left_other = refs[ends[index] : ends[index] + 1 + spans[index]]
            right, *others = refs[ends[index] + 1 + spans[index] : ends[index + 1]]
            left_other = joined(left_other)
            columns = right.shape[-1]
            away = joined(others[place * halves : (place + 1) * halves])[:, taken : taken + columns]
            taken += columns
            sums.append(dot(left[...], right[place], TN) + dot(left_other, away, TN))
        whole = sums[0] if pairs == 1 else jnp.concatenate(sums, axis=1)
        columns = whole.shape[1] // chunks
        for index in range(chunks):
            part = whole[:, index * columns : (index + 1) * columns]
            kind = BF16 if place else F32
            result = outs[2 * index + place]
            if not extra:
                result[...] = part.astype(kind)
                continue
            pack, pack_other = refs[ends[-1] : ends[-1] + 2]
            at = slice(index * columns, (index + 1) * columns)
            lines = [pack[:6, at] + pack_other[:6, at]]
            for first in (8 + place, 12 + place):
                lines.append(pack[first : first + 1, at] + pack_other[first + 2 : first + 3, at])
            lines.append(jnp.zeros((8, columns), F32))
            lines = jnp.concatenate(lines, axis=0).astype(kind)
            share = part.shape[0] // result.shape[0]
            for dest in range(result.shape[0]):
                result[dest, :share, :] = part[dest * share : (dest + 1) * share].astype(kind)
                result[dest, share:, :] = lines


def combine_kernel(bit, keep, keep_other, arrived, arrived_other, kept, sent):
    kept[0] = keep[0, 0] + arrived[0, 0].astype(F32)
    sent[0] = (keep_other[0, 0] + arrived_other[0, 0].astype(F32)).astype(sent.dtype)


def block(shape):
    return pl.BlockSpec(shape, lambda step: (0,) * len(shape))


def first_two(shape):
    return pl.BlockSpec((2,) + shape[1:], lambda step: (0, 0, 0))


def stepped(shape):
    return pl.BlockSpec((1,) + shape[1:], lambda step: (step,) + (0,) * (len(shape) - 1))


def near_spec(shape):
    return pl.BlockSpec((1,) + shape[1:], lambda step: (jnp.minimum(step, 1), 0, 0))


def in_hbm(values):
    return [pltpu.with_memory_space_constraint(v, pltpu.HBM) if v.size > 2**17 else v for v in values]


def call(kernel, name, steps, ins, outs, scratch, waits=(), cost=1, stay=False):
    count = len(ins)
    skip = count + len(waits)
    values = [value for value, kind in ins]
    if stay:
        values = in_hbm(values)

    def run(*refs):
        kernel(*refs[:count], *refs[skip:])

    return pl.pallas_call(
        run,
        grid=(steps,),
        in_specs=[kind(value.shape) for value, kind in ins] + [pl.BlockSpec(memory_space=pl.ANY)] * len(waits),
        out_specs=[kind(shape) for shape, dtype, kind in outs],
        out_shape=[jax.ShapeDtypeStruct(shape, dtype) for shape, dtype, kind in outs],
        scratch_shapes=scratch,
        compiler_params=pltpu.CompilerParams(vmem_limit_bytes=VMEM_BYTES),
        cost_estimate=pl.CostEstimate(flops=cost, bytes_accessed=cost, transcendentals=0),
        name=name,
    )(*values, *in_hbm(waits))


def attend(rows, segment, weight, bias, normed=None, first=None, waits=(), cost=1):
    steps = weight.shape[0]
    total, model = rows.shape
    width = bias.shape[-1] // 3
    ins = [(rows, block), (segment[:, None], block), (segment[None, :], block), (weight, stepped), (bias, stepped)]
    outs = [((total, model), F32, block)]
    if first is None:
        ins.append((normed, block))
    else:
        ins += [(v, block) for v in first]
        outs.append(((total, model), BF16, block))
    outs += [
        ((steps, total, 3 * width), BF16, stepped),
        ((steps, total, width), BF16, stepped),
        ((steps, 8, total), F32, stepped),
    ]
    return call(
        functools.partial(attend_kernel, first is not None), "attend", steps, ins, outs,
        [pltpu.VMEM((total, total), F32), pltpu.VMEM((total, model), F32)], waits, cost,
    )


def feed(rows, fc, out, b_fc, normed=None, first=None, last=None, keep=False, cost=1):
    steps = fc.shape[0]
    total, model = rows.shape
    units = fc.shape[-1]
    ins = [(rows, block), (fc, stepped), (out, stepped), (b_fc, stepped)]
    outs = [((total, model), F32 if last is None else BF16, block)]
    if first is None:
        ins.append((normed, block))
    else:
        ins += [(v, block) for v in first]
        outs.append(((total, model), BF16, block))
    if last is not None:
        ins += [(v, block) for v in last]
    if keep:
        outs += [
            ((steps, total, units), BF16, stepped),
            ((steps // 2, total, units), BF16, near_spec),
            ((total, units), BF16, block),
            ((total, units), BF16, block),
        ]
    return call(
        functools.partial(feed_kernel, first is not None, last is not None, keep), "feed", steps, ins, outs,
        [pltpu.VMEM((total, model), F32)], (), cost,
    )


def feed_back(grad, live, middle, slope, fc, out, gain, waits=(), cost=1, stay=False):
    steps = fc.shape[0]
    total, model = grad.shape
    units = fc.shape[-1]
    if stay:
        slope, fc, out = in_hbm((slope, fc, out))
    ins = [(grad, block), (live, block), (middle, block), (slope, stepped), (fc, stepped), (out, stepped), (gain, block)]
    outs = [
        ((total, model), F32, block),
        ((total, model), BF16, block),
        *[((total // 2, model), BF16, block)] * 2,
        ((total, model), BF16, block),
        ((steps // 2, total, units), BF16, near_spec),
        *[((total // 2, units), BF16, block)] * 4,
        ((steps, 1, units), F32, stepped),
        ((8, model), F32, block),
    ]
    return call(
        feed_back_kernel, "feed_back", steps, ins, outs, [pltpu.VMEM((total, model), F32)], waits, cost
    )


def attend_back(grad_attn, grad_middle, rows, segment, weight, mixed, context, logsum, gain, small_two, b_fc, waits=(), cost=1):
    steps = weight.shape[0]
    total, model = grad_attn.shape
    width = context.shape[-1]
    ins = [
        (grad_attn, block), (grad_middle, block), (rows, block), (segment[:, None], block), (segment[None, :], block),
        (weight, stepped), (mixed, stepped), (context, stepped), (logsum, stepped), (gain, block),
        (small_two, block), (b_fc, block),
    ]
    outs = [
        ((total, model), BF16, block),
        ((steps // 2, total, 3 * width), BF16, near_spec),
        *[((total // 2, 4 * width), BF16, block)] * 4,
        ((16, model), F32, block),
    ]
    return call(
        attend_back_kernel, "attend_back", steps, ins, outs,
        [pltpu.VMEM((total, total), F32), pltpu.VMEM((total, model), F32)], waits, cost,
    )


def outer(*pairs, chunks=1, packs=(), waits=()):
    ins, columns, spans = [], 0, []
    for left, left_other, right, others in pairs:
        ins += [(v, block) for v in (left, *left_other)] + [(right, first_two)] + [(v, block) for v in others]
        spans.append(len(left_other))
        halves = len(others) // 2
        columns += right.shape[-1]
    model = pairs[0][0].shape[1]
    groups = lax.axis_size("dp")
    shape = (groups, model // groups + 16, columns // chunks) if packs else (model, columns // chunks)
    outs = [(shape, F32, block), (shape, BF16, block)] * chunks
    ins += [(v, block) for v in packs]
    made = call(functools.partial(outer_kernel, len(pairs), chunks, spans, halves, bool(packs)), "outer", 1, ins, outs, [], waits, 1, True)
    return [list(made[2 * index : 2 * index + 2]) for index in range(chunks)]


def combine(keep, arrived, bit, kind, waits=()):
    pairs, unused, rows, columns = keep.shape

    def run(*refs):
        combine_kernel(*refs[:5], *refs[5 + len(waits) :])

    def spec(flip):
        return pl.BlockSpec((1, 1, rows, columns), lambda step, where: (step, flip + (1 - 2 * flip) * where[0], 0, 0))

    ends = pl.BlockSpec((1, rows, columns), lambda step, where: (step, 0, 0))
    return pl.pallas_call(
        run,
        grid_spec=pltpu.PrefetchScalarGridSpec(
            num_scalar_prefetch=1,
            grid=(pairs,),
            in_specs=[spec(0), spec(1), spec(0), spec(1)] + [pl.BlockSpec(memory_space=pl.ANY)] * len(waits),
            out_specs=[ends, ends],
        ),
        out_shape=[
            jax.ShapeDtypeStruct((pairs, rows, columns), F32),
            jax.ShapeDtypeStruct((pairs, rows, columns), kind),
        ],
        compiler_params=pltpu.CompilerParams(vmem_limit_bytes=VMEM_BYTES),
        cost_estimate=pl.CostEstimate(flops=1, bytes_accessed=1, transcendentals=0),
        name="combine",
    )(bit, keep, keep, arrived, arrived, *in_hbm(waits))


def partner(values, distance):
    return lax.ppermute(values, "tensor", [(i, i ^ distance) for i in range(4)])


def together(*values):
    return lax.optimization_barrier(values)


def dp_paired():
    return lax.axis_size("dp") % 2 == 0


def half_of(own, shared):
    odd = lax.axis_index("dp") & 1
    return lax.dynamic_slice_in_dim(own, odd * (shared // 2), shared // 2, 0)


def swapped(mine, rest):
    odd = (lax.axis_index("dp") & 1) == 1
    other = lax.ppermute(mine, "dp", [(i, i ^ 1) for i in range(lax.axis_size("dp"))])
    return jnp.concatenate([jnp.where(odd, other, mine), jnp.where(odd, mine, other)] + rest, axis=0)


def straight(pieces, index):
    odd = (index & 1) == 1
    upper = (index & 2) == 2
    low = [jnp.where(odd, pieces[k ^ 1], pieces[k]) for k in range(4)]
    return [jnp.where(upper, low[k ^ 2], low[k]) for k in range(4)]


def rows_to_batches(first, inputs, cotangent, index):
    pieces = []
    for k in range(4):
        both = [lax.dynamic_index_in_dim(v, index ^ k, 0, keepdims=False) for v in (inputs, cotangent)]
        pieces.append(jnp.where(first, both[0], both[1]))
    pieces = [pieces[0]] + [partner(pieces[k], k) for k in range(1, 4)]
    return jnp.concatenate(straight(pieces, index), axis=0)


def rows_sent(rows, index):
    own = rows.shape[0] // 4
    pieces = [lax.dynamic_slice_in_dim(rows, (index ^ k) * own, own, 0) for k in range(4)]
    return [pieces[0]] + [partner(pieces[k], k) for k in range(1, 4)]


def dp_stages():
    count = lax.axis_size("dp")
    return [1 << i for i in range(count.bit_length() - 1)] if count & (count - 1) == 0 else None


class Reduction:
    def __init__(self, keep, arriving, kind):
        self.keep, self.arriving, self.kind = keep, arriving, kind
        self.share = keep.shape[0] // lax.axis_size("dp")
        self.left = dp_stages()

    def begin(self, *waits):
        distance = self.left.pop(0)
        columns = self.keep.shape[-1]
        bit = (lax.axis_index("dp") // distance) & 1
        shape = (self.keep.size // (2 * columns * self.share), 2, self.share, columns)
        self.keep, sent = combine(
            self.keep.reshape(shape), self.arriving.reshape(shape), bit[None], self.kind, waits
        )
        total = lax.axis_size("dp")
        self.arriving = lax.ppermute(sent, "dp", [(i, i ^ distance) for i in range(total)])
        return sent

    def result(self, *waits):
        if self.left is None:
            whole = (self.keep + self.arriving.astype(F32)).astype(self.kind)
            return lax.psum_scatter(whole, "dp", scatter_dimension=0, tiled=True).astype(F32)
        while self.left:
            self.begin(*waits)
        whole = self.keep + self.arriving.astype(F32)
        return whole.reshape(whole.shape[-2:])


def body(
    inputs,
    cotangent,
    seq_lengths,
    w_attn,
    b_qv,
    w_proj,
    b_proj,
    w_fc,
    b_fc,
    w_out,
    b_out,
    ln_gain,
    ln_bias,
):
    micro, own, model = inputs.shape
    total = own * lax.axis_size("tensor")
    width = w_attn.shape[-1]
    groups = lax.axis_size("dp")
    me = lax.axis_index("tensor")
    first = lax.axis_index("section") == 0

    units = w_fc.shape[-1]
    shared = units // 3 if units % 96 == 0 else units
    unit_attn = jnp.concatenate([w_attn[0].reshape(model, 3 * width), w_proj[0].T], axis=1)
    paired = dp_paired()
    first_sent = half_of(unit_attn, model) if paired else unit_attn
    attn_far = partner(first_sent, 2)
    staged = rows_to_batches(first, inputs, cotangent, me)
    split_own = jnp.concatenate([b_qv[0, 0], jnp.zeros_like(b_qv[0, 0]), b_qv[0, 1], b_fc[0]])
    split_far = partner(split_own, 2)
    split_all = [split_own, partner(split_own, 1), split_far, partner(split_far, 1)]
    b_mixed = [v[None, None, : 3 * width].astype(F32) for v in split_all]
    b_fcs = [v[None, None, 3 * width :].astype(F32) for v in split_all]
    b_proj = b_proj.astype(F32)
    b_out = b_out.astype(F32)
    ln_gain = ln_gain[0].astype(F32)
    ln_bias = ln_bias[0].astype(F32)
    norm_one = (ln_gain[0:1], ln_bias[0:1], b_proj)
    norm_two = (ln_gain[1:2], ln_bias[1:2])

    lengths = lax.dynamic_index_in_dim(seq_lengths[0], me, 0, keepdims=False)
    ends = jnp.cumsum(lengths)
    position = jnp.arange(total, dtype=jnp.int32)
    segment = jnp.sum((position[:, None] >= ends[None, :]).astype(jnp.int32), axis=1)
    live = (position < ends[-1]).astype(F32)[:, None]
    last = (live, b_out)

    def attend_one(middle, k, normed, cost=1):
        return attend(middle, segment, attn[k][None], b_mixed[k], normed=normed, cost=cost)[0]

    def feed_one(result, k, normed, ending=None, cost=1):
        return feed(result, fc[k][None], out[k][None], b_fcs[k], normed=normed, last=ending, cost=cost)[0]

    attn = {0: unit_attn, 1: partner(unit_attn, 1)}
    fc = {0: w_fc[0], 1: partner(w_fc[0], 1)}
    out = {0: w_out[0], 1: partner(w_out[0], 1)}
    fc_far = partner(half_of(w_fc[0], model) if paired else w_fc[0], 2)
    middle, normed = attend(
        staged, segment, attn[0][None], b_mixed[0], first=norm_one, waits=split_all[2:], cost=MID
    )[:2]
    if paired:
        out_sent, rest, middle = together(half_of(w_out[0], shared), w_out[0, shared:], middle)
        out_far, rest = partner(out_sent, 2), [partner(rest, 2)] if shared < units else []
        attn_far, middle = together(attn_far, middle)
        attn_far = swapped(attn_far, [])
        fc_far, middle = together(fc_far, middle)
        fc_far = swapped(fc_far, [])
    else:
        out_sent, middle = together(w_out[0], middle)
        out_far = partner(out_sent, 2)
    middle = attend_one(middle, 1, normed, MID)
    if paired:
        out_far, middle = together(out_far, middle)
        out_far = swapped(out_far, rest)
    attn[2], attn[3] = attn_far, partner(attn_far, 1)
    middle = attend_one(middle, 2, normed, MID)
    middle = attend_one(middle, 3, normed, MID)
    fc_far, middle = together(fc_far, middle)
    result, normed = feed(middle, fc[0][None], out[0][None], b_fcs[0], first=norm_two, cost=MID)
    out_far, result = together(out_far, result)
    result = feed_one(result, 1, normed, cost=MID)
    fc[2], fc[3] = fc_far, partner(fc_far, 1)
    out[2], out[3] = out_far, partner(out_far, 1)
    result = feed_one(result, 2, normed)
    result = feed_one(result, 3, normed, last)
    received = lax.ppermute(result, "section", [(0, 1)])

    attn, fc, out, result = together(*[[v[k] for k in PLACES] for v in (attn, fc, out)], result)
    attn, fc, out = [jnp.stack(v) for v in (attn, fc, out)]
    b_mixed, b_fcs = [jnp.concatenate([v[k] for k in PLACES]) for v in (b_mixed, b_fcs)]
    rows = jnp.where(first, staged, received)
    middle, normed, mixed, context, logsum = attend(rows, segment, attn, b_mixed, first=norm_one, cost=LONG)
    result, normed_two, slope, active, *active_away = feed(
        middle, fc, out, b_fcs, first=norm_two, last=last, keep=True, cost=LONG
    )
    section_out = jnp.stack(straight(rows_sent(result, me), me))
    normed_other = partner(normed, 1)
    normed_two_other = partner(normed_two, 1)
    active_other = [partner(v, 1) for v in active_away]

    fed = feed_back(staged, live, middle, slope, fc, out, norm_two[0], cost=LONG)
    early = (normed_other, normed_two_other, *active_other)
    passed = attend_back(fed[1], fed[0], rows, segment, attn, mixed, context, logsum, norm_one[0], fed[-1], fed[-2], early, LONG)
    coming = lax.ppermute(passed[0], "section", [(1, 0)])
    grad_out = jnp.where(first, coming, staged)

    branch = (live * grad_out.astype(F32)).astype(BF16)
    ((keep_out, send_out),) = outer((branch, [partner(branch, 1)], active, active_other))
    sum_out = Reduction(keep_out, partner(send_out, 2), BF16)
    middle_grad, grad_attn, attn_high, attn_low, branch, hid, *hid_away, g_bfc, small_two = feed_back(
        grad_out, live, middle, slope, fc, out, norm_two[0], (send_out,), 1, True
    )
    grad_rows, mix, *mix_away, pack = attend_back(
        grad_attn, middle_grad, rows, segment, attn, mixed, context, logsum, norm_one[0], small_two, g_bfc
    )
    staggered = sum_out.left is not None
    if staggered:
        token = sum_out.begin(grad_rows)
        *hid_away, attn_high, attn_low, token = together(*hid_away, attn_high, attn_low, token)
    hid_other = [partner(v, 1) for v in hid_away]
    grad_attn_other = [partner(attn_high, 1), partner(attn_low, 1)]
    ((keep_fc, send_fc),) = outer((normed_two, [normed_two_other], hid, hid_other), waits=(section_out,))
    sum_fc = Reduction(keep_fc, partner(send_fc, 2), BF16)
    *mix_away, pack, token = together(*mix_away, pack, send_fc)
    pack_other = partner(pack, 1)
    mix_other = [partner(v, 1) for v in mix_away]
    kept = outer(
        (normed, [normed_other], mix, mix_other),
        (grad_attn, grad_attn_other, context, mix_other),
        chunks=2,
        packs=(pack, pack_other),
        waits=(token,),
    )
    kept = [[v.reshape(-1, v.shape[-1]) for v in pair] for pair in kept]
    sums_attn = [Reduction(keep, partner(send, 2), BF16) for keep, send in kept]
    if staggered:
        token = sum_out.begin(kept[0][1])
        token = sum_fc.begin(token)
        token = sums_attn[0].begin(token)
        grad_rows, token = together(grad_rows, token)
        input_grad = rows_sent(grad_rows, me)
        token = sum_fc.begin(token)
        token = sums_attn[1].begin(token)
        token = sums_attn[0].begin(token)
        token = sums_attn[1].begin(token)
        *input_grad, token = together(*input_grad, token)
    else:
        input_grad = rows_sent(grad_rows, me)
    input_grad = jnp.stack(straight(input_grad, me))
    g_out, g_fc = sum_out.result(), sum_fc.result()
    g_attn = [v.result() for v in sums_attn]
    g_attn = jnp.concatenate(g_attn, axis=1)

    g_attn, sums = g_attn[:-16], g_attn[-16:]
    g_wattn = g_attn[:, : 3 * width].reshape(-1, 3, width)
    g_wproj = g_attn[:, 3 * width :].T
    g_wout = g_out.T

    share = model // (groups * 4)
    g_bqv = sums[6, : 2 * width].reshape(2, width)
    g_bfc = sums[7]
    sums = lax.dynamic_slice_in_dim(sums, (lax.axis_index("dp") * 4 + me) * share, share, 1)
    return (
        section_out[None],
        input_grad[None],
        g_wattn[None],
        g_bqv[None],
        g_wproj[None],
        sums[4][None],
        g_fc[None],
        g_bfc[None],
        g_wout[None],
        sums[5][None],
        jnp.stack([sums[0], sums[2]])[None],
        jnp.stack([sums[1], sums[3]])[None],
    )


def solution(mesh):
    in_specs = (
        P(None, ("dp", "tensor"), None),
        P(None, ("dp", "tensor"), None),
        P("dp", None, None),
        P("section", None, None, "tensor"),
        P("section", None, "tensor"),
        P("section", "tensor", None),
        P("section", None),
        P("section", None, "tensor"),
        P("section", "tensor"),
        P("section", "tensor", None),
        P("section", None),
        P("section", None, None),
        P("section", None, None),
    )
    out_specs = (
        P("section", None, ("dp", "tensor"), None),
        P("section", None, ("dp", "tensor"), None),
        P("section", "dp", None, "tensor"),
        P("section", None, "tensor"),
        P("section", "tensor", "dp"),
        P("section", ("dp", "tensor")),
        P("section", "dp", "tensor"),
        P("section", "tensor"),
        P("section", "tensor", "dp"),
        P("section", ("dp", "tensor")),
        P("section", None, ("dp", "tensor")),
        P("section", None, ("dp", "tensor")),
    )
    return jax.shard_map(body, mesh=mesh, in_specs=in_specs, out_specs=out_specs, check_vma=False)
```

```python
import functools

import jax
import jax.numpy as jnp
from jax import lax
from jax.experimental import pallas as pl
from jax.experimental.pallas import tpu as pltpu
from jax.sharding import PartitionSpec as P

HEAD_DIM = 64
SCALE = HEAD_DIM**-0.5
F32 = jnp.float32
BF16 = jnp.bfloat16
PLACES = (0, 2, 1, 3)
GELU_A = (2.0 / jnp.pi) ** 0.5
GELU_B = 0.044715
VMEM_BYTES = 24 * 2**20
LONG = 10**10
MID = 1


def dot(left, right, dims):
    return lax.dot_general(left, right, (dims, ((), ())), preferred_element_type=F32)


NN = ((1,), (0,))
NT = ((1,), (1,))
TN = ((0,), (0,))


def normalized(rows):
    center = jnp.mean(rows, axis=-1, keepdims=True)
    centred = rows - center
    spread = lax.rsqrt(jnp.mean(centred * centred, axis=-1, keepdims=True) + 1e-05)
    return centred * spread, spread


def norm_back(rows, gain, grad):
    unit, spread = normalized(rows)
    scaled = grad * gain
    inner = jnp.mean(scaled * unit, axis=-1, keepdims=True)
    back = spread * (scaled - jnp.mean(scaled, axis=-1, keepdims=True) - unit * inner)
    return back, col_sum(grad * unit), col_sum(grad)


def col_sum(values):
    return jnp.sum(values, axis=0, keepdims=True)


def fill_mask(seg_col, seg_row, mask):
    total = mask.shape[0]
    key = lax.broadcasted_iota(jnp.int32, (total, total), 0)
    query = lax.broadcasted_iota(jnp.int32, (total, total), 1)
    allowed = (seg_col[...] == seg_row[...]) & (key <= query)
    mask[...] = jnp.where(allowed, 0.0, -1e30)


def bands(total):
    span = total // 2 if total % 256 == 0 else total
    return [(start, start + span) for start in range(0, total, span)]


def share_out(step, values, near, far):
    if near is not None:

        @pl.when(step < 2)
        def keep_near():
            near[0] = values

    for index, refs in enumerate(far):

        @pl.when(step == 2 + index)
        def keep_far(refs=refs):
            rows = values.shape[0] // len(refs)
            for part, ref in enumerate(refs):
                ref[...] = values[part * rows : (part + 1) * rows]


def attend_kernel(fresh, rows, seg_col, seg_row, weight, bias, *rest):
    if fresh:
        gain, shift, b_proj, total_out, normed_out, mixed_out, context_out, logsum_out, mask, total = rest
        normed = normed_out
    else:
        normed, total_out, mixed_out, context_out, logsum_out, mask, total = rest
    step = pl.program_id(0)
    width = context_out.shape[-1]
    count = rows.shape[0]

    @pl.when(step == 0)
    def start():
        fill_mask(seg_col, seg_row, mask)
        here = rows[...].astype(F32)
        if fresh:
            unit, unused = normalized(here)
            normed_out[...] = (unit * gain[...] + shift[...]).astype(BF16)
            total[...] = here + b_proj[...]
        else:
            total[...] = here

    wide = weight[0]
    mixed = (dot(normed[...], wide[:, : 3 * width], NN) + bias[0]).astype(BF16)
    mixed_out[0] = mixed
    pieces, stats = [], []
    for head in range(width // HEAD_DIM):
        at = head * HEAD_DIM
        queries = mixed[:, at : at + HEAD_DIM] * SCALE
        keys = mixed[:, width + at : width + at + HEAD_DIM]
        values = mixed[:, 2 * width + at : 2 * width + at + HEAD_DIM]
        made, logs = [], []
        for low, high in bands(count):
            scores = dot(keys[:high], queries[low:high], NT) + mask[:high, low:high]
            top = jnp.max(scores, axis=0, keepdims=True)
            expo = jnp.exp(scores - top)
            norm = jnp.sum(expo, axis=0, keepdims=True)
            made.append(dot(values[:high], expo.astype(BF16), TN) * (1.0 / norm))
            logs.append(top + jnp.log(norm))
        pieces.append(jnp.concatenate(made, axis=1))
        stats.append(jnp.concatenate(logs, axis=1))
    context = jnp.concatenate(pieces, axis=0).T.astype(BF16)
    context_out[0] = context
    stats.append(jnp.zeros((8 - len(stats), count), F32))
    logsum_out[0] = jnp.concatenate(stats, axis=0)
    total[...] += dot(context, wide[:, 3 * width :], NT)

    @pl.when(step == pl.num_programs(0) - 1)
    def finish():
        total_out[...] = total[...]


def feed_kernel(fresh, last, keep, rows, fc, out, b_fc, *rest):
    rest = list(rest)
    if fresh:
        gain, shift = rest[:2]
        rest = rest[2:]
    else:
        normed = rest.pop(0)
    if last:
        live, b_out = rest[:2]
        rest = rest[2:]
    result = rest.pop(0)
    if fresh:
        normed = rest.pop(0)
    if keep:
        slope_out, active_near, active_far = rest[0], rest[1], (rest[2:3], rest[3:4])
    total = rest[-1]
    step = pl.program_id(0)
    count = rows.shape[0]

    @pl.when(step == 0)
    def start():
        if fresh:
            unit, unused = normalized(rows[...])
            normed[...] = (unit * gain[...] + shift[...]).astype(BF16)
        total[...] = rows[...]

    made = []
    for low, high in bands(count):
        hidden = dot(normed[low:high, :], fc[0], NN) + b_fc[0]
        square = hidden * hidden
        tanh = jnp.tanh(GELU_A * hidden * (1.0 + GELU_B * square))
        upper = 0.5 * (1.0 + tanh)
        active = (hidden * upper).astype(BF16)
        total[low:high, :] += dot(active, out[0], NN)
        if keep:
            inner = GELU_A * hidden * (1.0 + 3.0 * GELU_B * square)
            slope_out[0, low:high, :] = (upper + upper * (1.0 - tanh) * inner).astype(BF16)
            made.append(active)
    if keep:
        share_out(step, jnp.concatenate(made, axis=0), active_near, active_far)

    @pl.when(step == pl.num_programs(0) - 1)
    def finish():
        if last:
            result[...] = (live[...] * (total[...] + b_out[...])).astype(BF16)
        else:
            result[...] = total[...]


def feed_back_kernel(
    grad, live, middle, slope, fc, out, gain, grad_middle, grad_attn, attn_high, attn_low, branch_out, near,
    far_one, far_one_low, far_two, far_two_low, b_fc_out, small, total,
):
    step = pl.program_id(0)
    count = grad.shape[0]

    @pl.when(step == 0)
    def start():
        branch_out[...] = (live[...] * grad[...].astype(F32)).astype(BF16)
        total[...] = jnp.zeros_like(total)

    bias_sum = 0.0
    made = []
    for low, high in bands(count):
        grad_active = dot(branch_out[low:high, :], out[0], NT)
        grad_hidden = (grad_active * slope[0, low:high, :].astype(F32)).astype(BF16)
        bias_sum = bias_sum + col_sum(grad_hidden.astype(F32))
        total[low:high, :] += dot(grad_hidden, fc[0], NT)
        made.append(grad_hidden)
    b_fc_out[0] = bias_sum
    share_out(step, jnp.concatenate(made, axis=0), near, ((far_one, far_one_low), (far_two, far_two_low)))

    @pl.when(step == pl.num_programs(0) - 1)
    def finish():
        back, gain_sum, shift_sum = norm_back(middle[...], gain[...], total[...])
        back = back + live[...] * grad[...].astype(F32)
        grad_middle[...] = back
        rounded = back.astype(BF16)
        grad_attn[...] = rounded
        attn_high[...] = rounded[: count // 2]
        attn_low[...] = rounded[count // 2 :]
        sums = [gain_sum, shift_sum, col_sum(rounded.astype(F32)), col_sum(branch_out[...].astype(F32))]
        small[...] = jnp.concatenate(sums + [jnp.zeros((4, gain_sum.shape[1]), F32)], axis=0)


def attend_back_kernel(
    grad_attn, grad_middle, rows, seg_col, seg_row, weight, mixed, context, logsum, gain, small_two, b_fc,
    grad_rows, near, far_one, far_one_low, far_two, far_two_low, pack, mask, total,
):
    step = pl.program_id(0)
    width = context.shape[-1]
    count = grad_attn.shape[0]

    @pl.when(step == 0)
    def start():
        fill_mask(seg_col, seg_row, mask)
        total[...] = jnp.zeros_like(total)

    wide = weight[0]
    grad_context = dot(grad_attn[...], wide[:, 3 * width :], NN).astype(BF16)
    product = (grad_context.astype(F32) * context[0].astype(F32)).T
    every = mixed[0]
    all_q, all_k, all_v = [], [], []
    for head in range(width // HEAD_DIM):
        at = head * HEAD_DIM
        queries = every[:, at : at + HEAD_DIM] * SCALE
        keys = every[:, width + at : width + at + HEAD_DIM]
        values = every[:, 2 * width + at : 2 * width + at + HEAD_DIM]
        grad = grad_context[:, at : at + HEAD_DIM]
        weighted = col_sum(product[at : at + HEAD_DIM, :])
        grad_q, grad_k, grad_v = [], [], []
        for low, high in bands(count):
            scores = dot(keys[:high], queries[low:high], NT) + mask[:high, low:high]
            probs = jnp.exp(scores - logsum[0, head : head + 1, low:high])
            grad_probs = dot(values[:high], grad[low:high], NT)
            grad_scores = (probs * (grad_probs - weighted[:, low:high])).astype(BF16)
            grad_v.append(dot(probs.astype(BF16), grad[low:high], NN))
            grad_k.append(dot(grad_scores, queries[low:high], NN))
            grad_q.append(dot(keys[:high], grad_scores, TN) * SCALE)
        for parts, whole in ((grad_k, all_k), (grad_v, all_v)):
            summed = parts[-1]
            for part in parts[:-1]:
                reach = part.shape[0]
                summed = jnp.concatenate([summed[:reach] + part, summed[reach:]], axis=0)
            whole.append(summed)
        all_q.append(jnp.concatenate(grad_q, axis=1))
    first = jnp.concatenate(all_q, axis=0).T
    grad_mixed = jnp.concatenate([first] + all_k + all_v, axis=1).astype(BF16)

    share_out(step, grad_mixed, near, ())
    both = jnp.concatenate([grad_mixed, context[0]], axis=1)
    share_out(step, both, None, ((far_one, far_one_low), (far_two, far_two_low)))
    sums = col_sum(grad_mixed.astype(F32))
    spare = jnp.zeros((1, pack.shape[-1] - 2 * width), F32)
    pack[pl.ds(8 + step, 1), :] = jnp.concatenate([sums[:, :width], sums[:, 2 * width :], spare], axis=1)
    total[...] += dot(grad_mixed, wide[:, : 3 * width], NT)

    @pl.when(step == pl.num_programs(0) - 1)
    def finish():
        back, gain_sum, shift_sum = norm_back(rows[...].astype(F32), gain[...], total[...])
        grad_rows[...] = (grad_middle[...] + back).astype(BF16)
        spare = jnp.zeros((2, gain_sum.shape[1]), F32)
        pack[:8, :] = jnp.concatenate([gain_sum, shift_sum, small_two[:4, :], spare], axis=0)
        pack[12:, :] = jnp.concatenate([b_fc[place] for place in range(4)], axis=0)


def joined(refs):
    values = [ref[...] for ref in refs]
    return jnp.concatenate(values, axis=0) if len(values) > 1 else values[0]


def outer_kernel(pairs, chunks, spans, halves, extra, *refs):
    ends = [sum(2 + span + 2 * halves for span in spans[:index]) for index in range(pairs + 1)]
    outs = refs[ends[-1] + 2 * extra :]
    for place in range(2):
        sums, taken = [], 0
        for index in range(pairs):
            left, *left_other = refs[ends[index] : ends[index] + 1 + spans[index]]
            right, *others = refs[ends[index] + 1 + spans[index] : ends[index + 1]]
            left_other = joined(left_other)
            columns = right.shape[-1]
            away = joined(others[place * halves : (place + 1) * halves])[:, taken : taken + columns]
            taken += columns
            sums.append(dot(left[...], right[place], TN) + dot(left_other, away, TN))
        whole = sums[0] if pairs == 1 else jnp.concatenate(sums, axis=1)
        columns = whole.shape[1] // chunks
        for index in range(chunks):
            part = whole[:, index * columns : (index + 1) * columns]
            kind = BF16 if place else F32
            result = outs[2 * index + place]
            if not extra:
                result[...] = part.astype(kind)
                continue
            pack, pack_other = refs[ends[-1] : ends[-1] + 2]
            at = slice(index * columns, (index + 1) * columns)
            lines = [pack[:6, at] + pack_other[:6, at]]
            for first in (8 + place, 12 + place):
                lines.append(pack[first : first + 1, at] + pack_other[first + 2 : first + 3, at])
            lines.append(jnp.zeros((8, columns), F32))
            lines = jnp.concatenate(lines, axis=0).astype(kind)
            share = part.shape[0] // result.shape[0]
            for dest in range(result.shape[0]):
                result[dest, :share, :] = part[dest * share : (dest + 1) * share].astype(kind)
                result[dest, share:, :] = lines


def combine_kernel(bit, keep, keep_other, arrived, arrived_other, kept, sent):
    kept[0] = keep[0, 0] + arrived[0, 0].astype(F32)
    sent[0] = (keep_other[0, 0] + arrived_other[0, 0].astype(F32)).astype(sent.dtype)


def block(shape):
    return pl.BlockSpec(shape, lambda step: (0,) * len(shape))


def first_two(shape):
    return pl.BlockSpec((2,) + shape[1:], lambda step: (0, 0, 0))


def stepped(shape):
    return pl.BlockSpec((1,) + shape[1:], lambda step: (step,) + (0,) * (len(shape) - 1))


def near_spec(shape):
    return pl.BlockSpec((1,) + shape[1:], lambda step: (jnp.minimum(step, 1), 0, 0))


def in_hbm(values):
    return [pltpu.with_memory_space_constraint(v, pltpu.HBM) if v.size > 2**17 else v for v in values]


def call(kernel, name, steps, ins, outs, scratch, waits=(), cost=1, stay=False):
    count = len(ins)
    skip = count + len(waits)
    values = [value for value, kind in ins]
    if stay:
        values = in_hbm(values)

    def run(*refs):
        kernel(*refs[:count], *refs[skip:])

    return pl.pallas_call(
        run,
        grid=(steps,),
        in_specs=[kind(value.shape) for value, kind in ins] + [pl.BlockSpec(memory_space=pl.ANY)] * len(waits),
        out_specs=[kind(shape) for shape, dtype, kind in outs],
        out_shape=[jax.ShapeDtypeStruct(shape, dtype) for shape, dtype, kind in outs],
        scratch_shapes=scratch,
        compiler_params=pltpu.CompilerParams(vmem_limit_bytes=VMEM_BYTES),
        cost_estimate=pl.CostEstimate(flops=cost, bytes_accessed=cost, transcendentals=0),
        name=name,
    )(*values, *in_hbm(waits))


def attend(rows, segment, weight, bias, normed=None, first=None, waits=(), cost=1):
    steps = weight.shape[0]
    total, model = rows.shape
    width = bias.shape[-1] // 3
    ins = [(rows, block), (segment[:, None], block), (segment[None, :], block), (weight, stepped), (bias, stepped)]
    outs = [((total, model), F32, block)]
    if first is None:
        ins.append((normed, block))
    else:
        ins += [(v, block) for v in first]
        outs.append(((total, model), BF16, block))
    outs += [
        ((steps, total, 3 * width), BF16, stepped),
        ((steps, total, width), BF16, stepped),
        ((steps, 8, total), F32, stepped),
    ]
    return call(
        functools.partial(attend_kernel, first is not None), "attend", steps, ins, outs,
        [pltpu.VMEM((total, total), F32), pltpu.VMEM((total, model), F32)], waits, cost,
    )


def feed(rows, fc, out, b_fc, normed=None, first=None, last=None, keep=False, cost=1):
    steps = fc.shape[0]
    total, model = rows.shape
    units = fc.shape[-1]
    ins = [(rows, block), (fc, stepped), (out, stepped), (b_fc, stepped)]
    outs = [((total, model), F32 if last is None else BF16, block)]
    if first is None:
        ins.append((normed, block))
    else:
        ins += [(v, block) for v in first]
        outs.append(((total, model), BF16, block))
    if last is not None:
        ins += [(v, block) for v in last]
    if keep:
        outs += [
            ((steps, total, units), BF16, stepped),
            ((steps // 2, total, units), BF16, near_spec),
            ((total, units), BF16, block),
            ((total, units), BF16, block),
        ]
    return call(
        functools.partial(feed_kernel, first is not None, last is not None, keep), "feed", steps, ins, outs,
        [pltpu.VMEM((total, model), F32)], (), cost,
    )


def feed_back(grad, live, middle, slope, fc, out, gain, waits=(), cost=1, stay=False):
    steps = fc.shape[0]
    total, model = grad.shape
    units = fc.shape[-1]
    if stay:
        slope, fc, out = in_hbm((slope, fc, out))
    ins = [(grad, block), (live, block), (middle, block), (slope, stepped), (fc, stepped), (out, stepped), (gain, block)]
    outs = [
        ((total, model), F32, block),
        ((total, model), BF16, block),
        *[((total // 2, model), BF16, block)] * 2,
        ((total, model), BF16, block),
        ((steps // 2, total, units), BF16, near_spec),
        *[((total // 2, units), BF16, block)] * 4,
        ((steps, 1, units), F32, stepped),
        ((8, model), F32, block),
    ]
    return call(
        feed_back_kernel, "feed_back", steps, ins, outs, [pltpu.VMEM((total, model), F32)], waits, cost
    )


def attend_back(grad_attn, grad_middle, rows, segment, weight, mixed, context, logsum, gain, small_two, b_fc, waits=(), cost=1):
    steps = weight.shape[0]
    total, model = grad_attn.shape
    width = context.shape[-1]
    ins = [
        (grad_attn, block), (grad_middle, block), (rows, block), (segment[:, None], block), (segment[None, :], block),
        (weight, stepped), (mixed, stepped), (context, stepped), (logsum, stepped), (gain, block),
        (small_two, block), (b_fc, block),
    ]
    outs = [
        ((total, model), BF16, block),
        ((steps // 2, total, 3 * width), BF16, near_spec),
        *[((total // 2, 4 * width), BF16, block)] * 4,
        ((16, model), F32, block),
    ]
    return call(
        attend_back_kernel, "attend_back", steps, ins, outs,
        [pltpu.VMEM((total, total), F32), pltpu.VMEM((total, model), F32)], waits, cost,
    )


def outer(*pairs, chunks=1, packs=(), waits=()):
    ins, columns, spans = [], 0, []
    for left, left_other, right, others in pairs:
        ins += [(v, block) for v in (left, *left_other)] + [(right, first_two)] + [(v, block) for v in others]
        spans.append(len(left_other))
        halves = len(others) // 2
        columns += right.shape[-1]
    model = pairs[0][0].shape[1]
    groups = lax.axis_size("dp")
    shape = (groups, model // groups + 16, columns // chunks) if packs else (model, columns // chunks)
    outs = [(shape, F32, block), (shape, BF16, block)] * chunks
    ins += [(v, block) for v in packs]
    made = call(functools.partial(outer_kernel, len(pairs), chunks, spans, halves, bool(packs)), "outer", 1, ins, outs, [], waits, 1, True)
    return [list(made[2 * index : 2 * index + 2]) for index in range(chunks)]


def combine(keep, arrived, bit, kind, waits=()):
    pairs, unused, rows, columns = keep.shape

    def run(*refs):
        combine_kernel(*refs[:5], *refs[5 + len(waits) :])

    def spec(flip):
        return pl.BlockSpec((1, 1, rows, columns), lambda step, where: (step, flip + (1 - 2 * flip) * where[0], 0, 0))

    ends = pl.BlockSpec((1, rows, columns), lambda step, where: (step, 0, 0))
    return pl.pallas_call(
        run,
        grid_spec=pltpu.PrefetchScalarGridSpec(
            num_scalar_prefetch=1,
            grid=(pairs,),
            in_specs=[spec(0), spec(1), spec(0), spec(1)] + [pl.BlockSpec(memory_space=pl.ANY)] * len(waits),
            out_specs=[ends, ends],
        ),
        out_shape=[
            jax.ShapeDtypeStruct((pairs, rows, columns), F32),
            jax.ShapeDtypeStruct((pairs, rows, columns), kind),
        ],
        compiler_params=pltpu.CompilerParams(vmem_limit_bytes=VMEM_BYTES),
        cost_estimate=pl.CostEstimate(flops=1, bytes_accessed=1, transcendentals=0),
        name="combine",
    )(bit, keep, keep, arrived, arrived, *in_hbm(waits))


def partner(values, distance):
    return lax.ppermute(values, "tensor", [(i, i ^ distance) for i in range(4)])


def together(*values):
    return lax.optimization_barrier(values)


def dp_paired():
    return lax.axis_size("dp") % 2 == 0


def half_of(own, shared):
    odd = lax.axis_index("dp") & 1
    return lax.dynamic_slice_in_dim(own, odd * (shared // 2), shared // 2, 0)


def swapped(mine, rest):
    odd = (lax.axis_index("dp") & 1) == 1
    other = lax.ppermute(mine, "dp", [(i, i ^ 1) for i in range(lax.axis_size("dp"))])
    return jnp.concatenate([jnp.where(odd, other, mine), jnp.where(odd, mine, other)] + rest, axis=0)


def straight(pieces, index):
    odd = (index & 1) == 1
    upper = (index & 2) == 2
    low = [jnp.where(odd, pieces[k ^ 1], pieces[k]) for k in range(4)]
    return [jnp.where(upper, low[k ^ 2], low[k]) for k in range(4)]


def rows_to_batches(first, inputs, cotangent, index):
    pieces = []
    for k in range(4):
        both = [lax.dynamic_index_in_dim(v, index ^ k, 0, keepdims=False) for v in (inputs, cotangent)]
        pieces.append(jnp.where(first, both[0], both[1]))
    pieces = [pieces[0]] + [partner(pieces[k], k) for k in range(1, 4)]
    return jnp.concatenate(straight(pieces, index), axis=0)


def rows_sent(rows, index):
    own = rows.shape[0] // 4
    pieces = [lax.dynamic_slice_in_dim(rows, (index ^ k) * own, own, 0) for k in range(4)]
    return [pieces[0]] + [partner(pieces[k], k) for k in range(1, 4)]


def dp_stages():
    count = lax.axis_size("dp")
    return [1 << i for i in range(count.bit_length() - 1)] if count & (count - 1) == 0 else None


class Reduction:
    def __init__(self, keep, arriving, kind):
        self.keep, self.arriving, self.kind = keep, arriving, kind
        self.share = keep.shape[0] // lax.axis_size("dp")
        self.left = dp_stages()

    def begin(self, *waits):
        distance = self.left.pop(0)
        columns = self.keep.shape[-1]
        bit = (lax.axis_index("dp") // distance) & 1
        shape = (self.keep.size // (2 * columns * self.share), 2, self.share, columns)
        self.keep, sent = combine(
            self.keep.reshape(shape), self.arriving.reshape(shape), bit[None], self.kind, waits
        )
        total = lax.axis_size("dp")
        self.arriving = lax.ppermute(sent, "dp", [(i, i ^ distance) for i in range(total)])
        return sent

    def result(self, *waits):
        if self.left is None:
            whole = (self.keep + self.arriving.astype(F32)).astype(self.kind)
            return lax.psum_scatter(whole, "dp", scatter_dimension=0, tiled=True).astype(F32)
        while self.left:
            self.begin(*waits)
        whole = self.keep + self.arriving.astype(F32)
        return whole.reshape(whole.shape[-2:])


def body(
    inputs,
    cotangent,
    seq_lengths,
    w_attn,
    b_qv,
    w_proj,
    b_proj,
    w_fc,
    b_fc,
    w_out,
    b_out,
    ln_gain,
    ln_bias,
):
    micro, own, model = inputs.shape
    total = own * lax.axis_size("tensor")
    width = w_attn.shape[-1]
    groups = lax.axis_size("dp")
    me = lax.axis_index("tensor")
    first = lax.axis_index("section") == 0

    units = w_fc.shape[-1]
    shared = units // 3 if units % 96 == 0 else units
    unit_attn = jnp.concatenate([w_attn[0].reshape(model, 3 * width), w_proj[0].T], axis=1)
    paired = dp_paired()
    first_sent = half_of(unit_attn, model) if paired else unit_attn
    attn_far = partner(first_sent, 2)
    staged = rows_to_batches(first, inputs, cotangent, me)
    split_own = jnp.concatenate([b_qv[0, 0], jnp.zeros_like(b_qv[0, 0]), b_qv[0, 1], b_fc[0]])
    split_far = partner(split_own, 2)
    split_all = [split_own, partner(split_own, 1), split_far, partner(split_far, 1)]
    b_mixed = [v[None, None, : 3 * width].astype(F32) for v in split_all]
    b_fcs = [v[None, None, 3 * width :].astype(F32) for v in split_all]
    b_proj = b_proj.astype(F32)
    b_out = b_out.astype(F32)
    ln_gain = ln_gain[0].astype(F32)
    ln_bias = ln_bias[0].astype(F32)
    norm_one = (ln_gain[0:1], ln_bias[0:1], b_proj)
    norm_two = (ln_gain[1:2], ln_bias[1:2])

    lengths = lax.dynamic_index_in_dim(seq_lengths[0], me, 0, keepdims=False)
    ends = jnp.cumsum(lengths)
    position = jnp.arange(total, dtype=jnp.int32)
    segment = jnp.sum((position[:, None] >= ends[None, :]).astype(jnp.int32), axis=1)
    live = (position < ends[-1]).astype(F32)[:, None]
    last = (live, b_out)

    def attend_one(middle, k, normed, cost=1):
        return attend(middle, segment, attn[k][None], b_mixed[k], normed=normed, cost=cost)[0]

    def feed_one(result, k, normed, ending=None, cost=1):
        return feed(result, fc[k][None], out[k][None], b_fcs[k], normed=normed, last=ending, cost=cost)[0]

    attn = {0: unit_attn, 1: partner(unit_attn, 1)}
    fc = {0: w_fc[0], 1: partner(w_fc[0], 1)}
    out = {0: w_out[0], 1: partner(w_out[0], 1)}
    fc_far = partner(half_of(w_fc[0], model) if paired else w_fc[0], 2)
    middle, normed = attend(
        staged, segment, attn[0][None], b_mixed[0], first=norm_one, waits=split_all[2:], cost=MID
    )[:2]
    if paired:
        out_sent, rest, middle = together(half_of(w_out[0], shared), w_out[0, shared:], middle)
        out_far, rest = partner(out_sent, 2), [partner(rest, 2)] if shared < units else []
        attn_far, middle = together(attn_far, middle)
        attn_far = swapped(attn_far, [])
        fc_far, middle = together(fc_far, middle)
        fc_far = swapped(fc_far, [])
    else:
        out_sent, middle = together(w_out[0], middle)
        out_far = partner(out_sent, 2)
    middle = attend_one(middle, 1, normed, MID)
    if paired:
        out_far, middle = together(out_far, middle)
        out_far = swapped(out_far, rest)
    attn[2], attn[3] = attn_far, partner(attn_far, 1)
    middle = attend_one(middle, 2, normed, MID)
    middle = attend_one(middle, 3, normed, MID)
    fc_far, middle = together(fc_far, middle)
    result, normed = feed(middle, fc[0][None], out[0][None], b_fcs[0], first=norm_two, cost=MID)
    out_far, result = together(out_far, result)
    result = feed_one(result, 1, normed, cost=MID)
    fc[2], fc[3] = fc_far, partner(fc_far, 1)
    out[2], out[3] = out_far, partner(out_far, 1)
    result = feed_one(result, 2, normed)
    result = feed_one(result, 3, normed, last)
    received = lax.ppermute(result, "section", [(0, 1)])

    attn, fc, out, result = together(*[[v[k] for k in PLACES] for v in (attn, fc, out)], result)
    attn, fc, out = [jnp.stack(v) for v in (attn, fc, out)]
    b_mixed, b_fcs = [jnp.concatenate([v[k] for k in PLACES]) for v in (b_mixed, b_fcs)]
    rows = jnp.where(first, staged, received)
    middle, normed, mixed, context, logsum = attend(rows, segment, attn, b_mixed, first=norm_one, cost=LONG)
    result, normed_two, slope, active, *active_away = feed(
        middle, fc, out, b_fcs, first=norm_two, last=last, keep=True, cost=LONG
    )
    section_out = rows_sent(result, me)
    normed_other = partner(normed, 1)
    normed_two_other = partner(normed_two, 1)
    active_other = [partner(v, 1) for v in active_away]

    fed = feed_back(staged, live, middle, slope, fc, out, norm_two[0], cost=LONG)
    early = (normed_other, normed_two_other, *active_other)
    passed = attend_back(fed[1], fed[0], rows, segment, attn, mixed, context, logsum, norm_one[0], fed[-1], fed[-2], early, LONG)
    coming = lax.ppermute(passed[0], "section", [(1, 0)])
    grad_out = jnp.where(first, coming, staged)

    branch = (live * grad_out.astype(F32)).astype(BF16)
    ((keep_out, send_out),) = outer((branch, [partner(branch, 1)], active, active_other))
    sum_out = Reduction(keep_out, partner(send_out, 2), BF16)
    middle_grad, grad_attn, attn_high, attn_low, branch, hid, *hid_away, g_bfc, small_two = feed_back(
        grad_out, live, middle, slope, fc, out, norm_two[0], (send_out,), 1, True
    )
    grad_rows, mix, *mix_away, pack = attend_back(
        grad_attn, middle_grad, rows, segment, attn, mixed, context, logsum, norm_one[0], small_two, g_bfc
    )
    *section_out, grad_rows = together(*section_out, grad_rows)
    section_out = jnp.stack(straight(section_out, me))
    staggered = sum_out.left is not None
    ready = []
    if staggered:
        ready = [sum_out.begin(grad_rows)]
    hid_other = [partner(v, 1) for v in hid_away]
    grad_attn_other = [partner(attn_high, 1), partner(attn_low, 1)]
    ((keep_fc, send_fc),) = outer((normed_two, [normed_two_other], hid, hid_other), waits=(section_out, *ready))
    sum_fc = Reduction(keep_fc, partner(send_fc, 2), BF16)
    pack_other = partner(pack, 1)
    mix_other = [partner(v, 1) for v in mix_away]
    kept = outer(
        (normed, [normed_other], mix, mix_other),
        (grad_attn, grad_attn_other, context, mix_other),
        chunks=2,
        packs=(pack, pack_other),
        waits=(send_fc,),
    )
    kept = [[v.reshape(-1, v.shape[-1]) for v in pair] for pair in kept]
    sums_attn = [Reduction(keep, partner(send, 2), BF16) for keep, send in kept]
    if staggered:
        token = sum_out.begin(kept[0][1])
        token = sum_fc.begin(token)
        token = sums_attn[0].begin(token)
        grad_rows, token = together(grad_rows, token)
        input_grad = rows_sent(grad_rows, me)
        token = sum_fc.begin(token)
        token = sums_attn[1].begin(token)
        g_fc = sum_fc.result()
        token = sums_attn[0].begin(token, g_fc)
        token = sums_attn[1].begin(token)
        *input_grad, token = together(*input_grad, token)
    else:
        input_grad = rows_sent(grad_rows, me)
        g_fc = sum_fc.result()
    input_grad = jnp.stack(straight(input_grad, me))
    g_out = sum_out.result()
    g_attn = [v.result() for v in sums_attn]
    g_attn = jnp.concatenate(g_attn, axis=1)

    g_attn, sums = g_attn[:-16], g_attn[-16:]
    g_wattn = g_attn[:, : 3 * width].reshape(-1, 3, width)
    g_wproj = g_attn[:, 3 * width :].T
    g_wout = g_out.T

    share = model // (groups * 4)
    g_bqv = sums[6, : 2 * width].reshape(2, width)
    g_bfc = sums[7]
    sums = lax.dynamic_slice_in_dim(sums, (lax.axis_index("dp") * 4 + me) * share, share, 1)
    return (
        section_out[None],
        input_grad[None],
        g_wattn[None],
        g_bqv[None],
        g_wproj[None],
        sums[4][None],
        g_fc[None],
        g_bfc[None],
        g_wout[None],
        sums[5][None],
        jnp.stack([sums[0], sums[2]])[None],
        jnp.stack([sums[1], sums[3]])[None],
    )


def solution(mesh):
    in_specs = (
        P(None, ("dp", "tensor"), None),
        P(None, ("dp", "tensor"), None),
        P("dp", None, None),
        P("section", None, None, "tensor"),
        P("section", None, "tensor"),
        P("section", "tensor", None),
        P("section", None),
        P("section", None, "tensor"),
        P("section", "tensor"),
        P("section", "tensor", None),
        P("section", None),
        P("section", None, None),
        P("section", None, None),
    )
    out_specs = (
        P("section", None, ("dp", "tensor"), None),
        P("section", None, ("dp", "tensor"), None),
        P("section", "dp", None, "tensor"),
        P("section", None, "tensor"),
        P("section", "tensor", "dp"),
        P("section", ("dp", "tensor")),
        P("section", "dp", "tensor"),
        P("section", "tensor"),
        P("section", "tensor", "dp"),
        P("section", ("dp", "tensor")),
        P("section", None, ("dp", "tensor")),
        P("section", None, ("dp", "tensor")),
    )
    return jax.shard_map(body, mesh=mesh, in_specs=in_specs, out_specs=out_specs, check_vma=False)
```

```python
import functools

import jax
import jax.numpy as jnp
from jax import lax
from jax.experimental import pallas as pl
from jax.experimental.pallas import tpu as pltpu
from jax.sharding import PartitionSpec as P

HEAD_DIM = 64
SCALE = HEAD_DIM**-0.5
F32 = jnp.float32
BF16 = jnp.bfloat16
PLACES = (0, 2, 1, 3)
GELU_A = (2.0 / jnp.pi) ** 0.5
GELU_B = 0.044715
VMEM_BYTES = 24 * 2**20
LONG = 10**10
MID = 1


def dot(left, right, dims):
    return lax.dot_general(left, right, (dims, ((), ())), preferred_element_type=F32)


NN = ((1,), (0,))
NT = ((1,), (1,))
TN = ((0,), (0,))


def normalized(rows):
    center = jnp.mean(rows, axis=-1, keepdims=True)
    centred = rows - center
    spread = lax.rsqrt(jnp.mean(centred * centred, axis=-1, keepdims=True) + 1e-05)
    return centred * spread, spread


def norm_back(rows, gain, grad):
    unit, spread = normalized(rows)
    scaled = grad * gain
    inner = jnp.mean(scaled * unit, axis=-1, keepdims=True)
    back = spread * (scaled - jnp.mean(scaled, axis=-1, keepdims=True) - unit * inner)
    return back, col_sum(grad * unit), col_sum(grad)


def col_sum(values):
    return jnp.sum(values, axis=0, keepdims=True)


def fill_mask(seg_col, seg_row, mask):
    total = mask.shape[0]
    key = lax.broadcasted_iota(jnp.int32, (total, total), 0)
    query = lax.broadcasted_iota(jnp.int32, (total, total), 1)
    allowed = (seg_col[...] == seg_row[...]) & (key <= query)
    mask[...] = jnp.where(allowed, 0.0, -1e30)


def bands(total):
    span = total // 2 if total % 256 == 0 else total
    return [(start, start + span) for start in range(0, total, span)]


def share_out(step, values, near, far):
    if near is not None:

        @pl.when(step < 2)
        def keep_near():
            near[0] = values

    for index, refs in enumerate(far):

        @pl.when(step == 2 + index)
        def keep_far(refs=refs):
            rows = values.shape[0] // len(refs)
            for part, ref in enumerate(refs):
                ref[...] = values[part * rows : (part + 1) * rows]


def attend_kernel(fresh, rows, seg_col, seg_row, weight, bias, *rest):
    if fresh:
        gain, shift, b_proj, total_out, normed_out, mixed_out, context_out, logsum_out, mask, total = rest
        normed = normed_out
    else:
        normed, total_out, mixed_out, context_out, logsum_out, mask, total = rest
    step = pl.program_id(0)
    width = context_out.shape[-1]
    count = rows.shape[0]

    @pl.when(step == 0)
    def start():
        fill_mask(seg_col, seg_row, mask)
        here = rows[...].astype(F32)
        if fresh:
            unit, unused = normalized(here)
            normed_out[...] = (unit * gain[...] + shift[...]).astype(BF16)
            total[...] = here + b_proj[...]
        else:
            total[...] = here

    wide = weight[0]
    mixed = (dot(normed[...], wide[:, : 3 * width], NN) + bias[0]).astype(BF16)
    mixed_out[0] = mixed
    pieces, stats = [], []
    for head in range(width // HEAD_DIM):
        at = head * HEAD_DIM
        queries = mixed[:, at : at + HEAD_DIM] * SCALE
        keys = mixed[:, width + at : width + at + HEAD_DIM]
        values = mixed[:, 2 * width + at : 2 * width + at + HEAD_DIM]
        made, logs = [], []
        for low, high in bands(count):
            scores = dot(keys[:high], queries[low:high], NT) + mask[:high, low:high]
            top = jnp.max(scores, axis=0, keepdims=True)
            expo = jnp.exp(scores - top)
            norm = jnp.sum(expo, axis=0, keepdims=True)
            made.append(dot(values[:high], expo.astype(BF16), TN) * (1.0 / norm))
            logs.append(top + jnp.log(norm))
        pieces.append(jnp.concatenate(made, axis=1))
        stats.append(jnp.concatenate(logs, axis=1))
    context = jnp.concatenate(pieces, axis=0).T.astype(BF16)
    context_out[0] = context
    stats.append(jnp.zeros((8 - len(stats), count), F32))
    logsum_out[0] = jnp.concatenate(stats, axis=0)
    total[...] += dot(context, wide[:, 3 * width :], NT)

    @pl.when(step == pl.num_programs(0) - 1)
    def finish():
        total_out[...] = total[...]


def feed_kernel(fresh, last, keep, rows, fc, out, b_fc, *rest):
    rest = list(rest)
    if fresh:
        gain, shift = rest[:2]
        rest = rest[2:]
    else:
        normed = rest.pop(0)
    if last:
        live, b_out = rest[:2]
        rest = rest[2:]
    result = rest.pop(0)
    if fresh:
        normed = rest.pop(0)
    if keep:
        slope_out, active_near, active_far = rest[0], rest[1], (rest[2:3], rest[3:4])
    total = rest[-1]
    step = pl.program_id(0)
    count = rows.shape[0]

    @pl.when(step == 0)
    def start():
        if fresh:
            unit, unused = normalized(rows[...])
            normed[...] = (unit * gain[...] + shift[...]).astype(BF16)
        total[...] = rows[...]

    made = []
    for low, high in bands(count):
        hidden = dot(normed[low:high, :], fc[0], NN) + b_fc[0]
        square = hidden * hidden
        tanh = jnp.tanh(GELU_A * hidden * (1.0 + GELU_B * square))
        upper = 0.5 * (1.0 + tanh)
        active = (hidden * upper).astype(BF16)
        total[low:high, :] += dot(active, out[0], NN)
        if keep:
            inner = GELU_A * hidden * (1.0 + 3.0 * GELU_B * square)
            slope_out[0, low:high, :] = (upper + upper * (1.0 - tanh) * inner).astype(BF16)
            made.append(active)
    if keep:
        share_out(step, jnp.concatenate(made, axis=0), active_near, active_far)

    @pl.when(step == pl.num_programs(0) - 1)
    def finish():
        if last:
            result[...] = (live[...] * (total[...] + b_out[...])).astype(BF16)
        else:
            result[...] = total[...]


def feed_back_kernel(
    grad, live, middle, slope, fc, out, gain, grad_middle, grad_attn, attn_high, attn_low, branch_out, near,
    far_one, far_one_low, far_two, far_two_low, b_fc_out, small, total,
):
    step = pl.program_id(0)
    count = grad.shape[0]

    @pl.when(step == 0)
    def start():
        branch_out[...] = (live[...] * grad[...].astype(F32)).astype(BF16)
        total[...] = jnp.zeros_like(total)

    bias_sum = 0.0
    made = []
    for low, high in bands(count):
        grad_active = dot(branch_out[low:high, :], out[0], NT)
        grad_hidden = (grad_active * slope[0, low:high, :].astype(F32)).astype(BF16)
        bias_sum = bias_sum + col_sum(grad_hidden.astype(F32))
        total[low:high, :] += dot(grad_hidden, fc[0], NT)
        made.append(grad_hidden)
    b_fc_out[0] = bias_sum
    share_out(step, jnp.concatenate(made, axis=0), near, ((far_one, far_one_low), (far_two, far_two_low)))

    @pl.when(step == pl.num_programs(0) - 1)
    def finish():
        back, gain_sum, shift_sum = norm_back(middle[...], gain[...], total[...])
        back = back + live[...] * grad[...].astype(F32)
        grad_middle[...] = back
        rounded = back.astype(BF16)
        grad_attn[...] = rounded
        attn_high[...] = rounded[: count // 2]
        attn_low[...] = rounded[count // 2 :]
        sums = [gain_sum, shift_sum, col_sum(rounded.astype(F32)), col_sum(branch_out[...].astype(F32))]
        small[...] = jnp.concatenate(sums + [jnp.zeros((4, gain_sum.shape[1]), F32)], axis=0)


def attend_back_kernel(
    grad_attn, grad_middle, rows, seg_col, seg_row, weight, mixed, context, logsum, gain, small_two, b_fc,
    grad_rows, near, far_one, far_one_low, far_two, far_two_low, pack, mask, total,
):
    step = pl.program_id(0)
    width = context.shape[-1]
    count = grad_attn.shape[0]

    @pl.when(step == 0)
    def start():
        fill_mask(seg_col, seg_row, mask)
        total[...] = jnp.zeros_like(total)

    wide = weight[0]
    grad_context = dot(grad_attn[...], wide[:, 3 * width :], NN).astype(BF16)
    product = (grad_context.astype(F32) * context[0].astype(F32)).T
    every = mixed[0]
    all_q, all_k, all_v = [], [], []
    for head in range(width // HEAD_DIM):
        at = head * HEAD_DIM
        queries = every[:, at : at + HEAD_DIM] * SCALE
        keys = every[:, width + at : width + at + HEAD_DIM]
        values = every[:, 2 * width + at : 2 * width + at + HEAD_DIM]
        grad = grad_context[:, at : at + HEAD_DIM]
        weighted = col_sum(product[at : at + HEAD_DIM, :])
        grad_q, grad_k, grad_v = [], [], []
        for low, high in bands(count):
            scores = dot(keys[:high], queries[low:high], NT) + mask[:high, low:high]
            probs = jnp.exp(scores - logsum[0, head : head + 1, low:high])
            grad_probs = dot(values[:high], grad[low:high], NT)
            grad_scores = (probs * (grad_probs - weighted[:, low:high])).astype(BF16)
            grad_v.append(dot(probs.astype(BF16), grad[low:high], NN))
            grad_k.append(dot(grad_scores, queries[low:high], NN))
            grad_q.append(dot(keys[:high], grad_scores, TN) * SCALE)
        for parts, whole in ((grad_k, all_k), (grad_v, all_v)):
            summed = parts[-1]
            for part in parts[:-1]:
                reach = part.shape[0]
                summed = jnp.concatenate([summed[:reach] + part, summed[reach:]], axis=0)
            whole.append(summed)
        all_q.append(jnp.concatenate(grad_q, axis=1))
    first = jnp.concatenate(all_q, axis=0).T
    grad_mixed = jnp.concatenate([first] + all_k + all_v, axis=1).astype(BF16)

    share_out(step, grad_mixed, near, ())
    both = jnp.concatenate([grad_mixed, context[0]], axis=1)
    share_out(step, both, None, ((far_one, far_one_low), (far_two, far_two_low)))
    sums = col_sum(grad_mixed.astype(F32))
    spare = jnp.zeros((1, pack.shape[-1] - 2 * width), F32)
    pack[pl.ds(8 + step, 1), :] = jnp.concatenate([sums[:, :width], sums[:, 2 * width :], spare], axis=1)
    total[...] += dot(grad_mixed, wide[:, : 3 * width], NT)

    @pl.when(step == pl.num_programs(0) - 1)
    def finish():
        back, gain_sum, shift_sum = norm_back(rows[...].astype(F32), gain[...], total[...])
        grad_rows[...] = (grad_middle[...] + back).astype(BF16)
        spare = jnp.zeros((2, gain_sum.shape[1]), F32)
        pack[:8, :] = jnp.concatenate([gain_sum, shift_sum, small_two[:4, :], spare], axis=0)
        pack[12:, :] = jnp.concatenate([b_fc[place] for place in range(4)], axis=0)


def joined(refs):
    values = [ref[...] for ref in refs]
    return jnp.concatenate(values, axis=0) if len(values) > 1 else values[0]


def outer_kernel(pairs, chunks, spans, halves, extra, *refs):
    ends = [sum(2 + span + 2 * halves for span in spans[:index]) for index in range(pairs + 1)]
    outs = refs[ends[-1] + 2 * extra :]
    for place in range(2):
        sums, taken = [], 0
        for index in range(pairs):
            left, *left_other = refs[ends[index] : ends[index] + 1 + spans[index]]
            right, *others = refs[ends[index] + 1 + spans[index] : ends[index + 1]]
            left_other = joined(left_other)
            columns = right.shape[-1]
            away = joined(others[place * halves : (place + 1) * halves])[:, taken : taken + columns]
            taken += columns
            sums.append(dot(left[...], right[place], TN) + dot(left_other, away, TN))
        whole = sums[0] if pairs == 1 else jnp.concatenate(sums, axis=1)
        columns = whole.shape[1] // chunks
        for index in range(chunks):
            part = whole[:, index * columns : (index + 1) * columns]
            kind = BF16 if place else F32
            result = outs[2 * index + place]
            if not extra:
                result[...] = part.astype(kind)
                continue
            pack, pack_other = refs[ends[-1] : ends[-1] + 2]
            at = slice(index * columns, (index + 1) * columns)
            lines = [pack[:6, at] + pack_other[:6, at]]
            for first in (8 + place, 12 + place):
                lines.append(pack[first : first + 1, at] + pack_other[first + 2 : first + 3, at])
            lines.append(jnp.zeros((8, columns), F32))
            lines = jnp.concatenate(lines, axis=0).astype(kind)
            share = part.shape[0] // result.shape[0]
            for dest in range(result.shape[0]):
                result[dest, :share, :] = part[dest * share : (dest + 1) * share].astype(kind)
                result[dest, share:, :] = lines


def combine_kernel(bit, keep, keep_other, arrived, arrived_other, kept, sent):
    kept[0] = keep[0, 0] + arrived[0, 0].astype(F32)
    sent[0] = (keep_other[0, 0] + arrived_other[0, 0].astype(F32)).astype(sent.dtype)


def block(shape):
    return pl.BlockSpec(shape, lambda step: (0,) * len(shape))


def first_two(shape):
    return pl.BlockSpec((2,) + shape[1:], lambda step: (0, 0, 0))


def stepped(shape):
    return pl.BlockSpec((1,) + shape[1:], lambda step: (step,) + (0,) * (len(shape) - 1))


def near_spec(shape):
    return pl.BlockSpec((1,) + shape[1:], lambda step: (jnp.minimum(step, 1), 0, 0))


def in_hbm(values):
    return [pltpu.with_memory_space_constraint(v, pltpu.HBM) if v.size > 2**17 else v for v in values]


def call(kernel, name, steps, ins, outs, scratch, waits=(), cost=1, stay=False):
    count = len(ins)
    skip = count + len(waits)
    values = [value for value, kind in ins]
    if stay:
        values = in_hbm(values)

    def run(*refs):
        kernel(*refs[:count], *refs[skip:])

    return pl.pallas_call(
        run,
        grid=(steps,),
        in_specs=[kind(value.shape) for value, kind in ins] + [pl.BlockSpec(memory_space=pl.ANY)] * len(waits),
        out_specs=[kind(shape) for shape, dtype, kind in outs],
        out_shape=[jax.ShapeDtypeStruct(shape, dtype) for shape, dtype, kind in outs],
        scratch_shapes=scratch,
        compiler_params=pltpu.CompilerParams(vmem_limit_bytes=VMEM_BYTES),
        cost_estimate=pl.CostEstimate(flops=cost, bytes_accessed=cost, transcendentals=0),
        name=name,
    )(*values, *in_hbm(waits))


def attend(rows, segment, weight, bias, normed=None, first=None, waits=(), cost=1):
    steps = weight.shape[0]
    total, model = rows.shape
    width = bias.shape[-1] // 3
    ins = [(rows, block), (segment[:, None], block), (segment[None, :], block), (weight, stepped), (bias, stepped)]
    outs = [((total, model), F32, block)]
    if first is None:
        ins.append((normed, block))
    else:
        ins += [(v, block) for v in first]
        outs.append(((total, model), BF16, block))
    outs += [
        ((steps, total, 3 * width), BF16, stepped),
        ((steps, total, width), BF16, stepped),
        ((steps, 8, total), F32, stepped),
    ]
    return call(
        functools.partial(attend_kernel, first is not None), "attend", steps, ins, outs,
        [pltpu.VMEM((total, total), F32), pltpu.VMEM((total, model), F32)], waits, cost,
    )


def feed(rows, fc, out, b_fc, normed=None, first=None, last=None, keep=False, cost=1):
    steps = fc.shape[0]
    total, model = rows.shape
    units = fc.shape[-1]
    ins = [(rows, block), (fc, stepped), (out, stepped), (b_fc, stepped)]
    outs = [((total, model), F32 if last is None else BF16, block)]
    if first is None:
        ins.append((normed, block))
    else:
        ins += [(v, block) for v in first]
        outs.append(((total, model), BF16, block))
    if last is not None:
        ins += [(v, block) for v in last]
    if keep:
        outs += [
            ((steps, total, units), BF16, stepped),
            ((steps // 2, total, units), BF16, near_spec),
            ((total, units), BF16, block),
            ((total, units), BF16, block),
        ]
    return call(
        functools.partial(feed_kernel, first is not None, last is not None, keep), "feed", steps, ins, outs,
        [pltpu.VMEM((total, model), F32)], (), cost,
    )


def feed_back(grad, live, middle, slope, fc, out, gain, waits=(), cost=1, stay=False):
    steps = fc.shape[0]
    total, model = grad.shape
    units = fc.shape[-1]
    if stay:
        slope, fc, out = in_hbm((slope, fc, out))
    ins = [(grad, block), (live, block), (middle, block), (slope, stepped), (fc, stepped), (out, stepped), (gain, block)]
    outs = [
        ((total, model), F32, block),
        ((total, model), BF16, block),
        *[((total // 2, model), BF16, block)] * 2,
        ((total, model), BF16, block),
        ((steps // 2, total, units), BF16, near_spec),
        *[((total // 2, units), BF16, block)] * 4,
        ((steps, 1, units), F32, stepped),
        ((8, model), F32, block),
    ]
    return call(
        feed_back_kernel, "feed_back", steps, ins, outs, [pltpu.VMEM((total, model), F32)], waits, cost
    )


def attend_back(grad_attn, grad_middle, rows, segment, weight, mixed, context, logsum, gain, small_two, b_fc, waits=(), cost=1):
    steps = weight.shape[0]
    total, model = grad_attn.shape
    width = context.shape[-1]
    ins = [
        (grad_attn, block), (grad_middle, block), (rows, block), (segment[:, None], block), (segment[None, :], block),
        (weight, stepped), (mixed, stepped), (context, stepped), (logsum, stepped), (gain, block),
        (small_two, block), (b_fc, block),
    ]
    outs = [
        ((total, model), BF16, block),
        ((steps // 2, total, 3 * width), BF16, near_spec),
        *[((total // 2, 4 * width), BF16, block)] * 4,
        ((16, model), F32, block),
    ]
    return call(
        attend_back_kernel, "attend_back", steps, ins, outs,
        [pltpu.VMEM((total, total), F32), pltpu.VMEM((total, model), F32)], waits, cost,
    )


def outer(*pairs, chunks=1, packs=(), waits=()):
    ins, columns, spans = [], 0, []
    for left, left_other, right, others in pairs:
        ins += [(v, block) for v in (left, *left_other)] + [(right, first_two)] + [(v, block) for v in others]
        spans.append(len(left_other))
        halves = len(others) // 2
        columns += right.shape[-1]
    model = pairs[0][0].shape[1]
    groups = lax.axis_size("dp")
    shape = (groups, model // groups + 16, columns // chunks) if packs else (model, columns // chunks)
    outs = [(shape, F32, block), (shape, BF16, block)] * chunks
    ins += [(v, block) for v in packs]
    made = call(functools.partial(outer_kernel, len(pairs), chunks, spans, halves, bool(packs)), "outer", 1, ins, outs, [], waits, 1, True)
    return [list(made[2 * index : 2 * index + 2]) for index in range(chunks)]


def combine(keep, arrived, bit, kind, waits=()):
    pairs, unused, rows, columns = keep.shape

    def run(*refs):
        combine_kernel(*refs[:5], *refs[5 + len(waits) :])

    def spec(flip):
        return pl.BlockSpec((1, 1, rows, columns), lambda step, where: (step, flip + (1 - 2 * flip) * where[0], 0, 0))

    ends = pl.BlockSpec((1, rows, columns), lambda step, where: (step, 0, 0))
    return pl.pallas_call(
        run,
        grid_spec=pltpu.PrefetchScalarGridSpec(
            num_scalar_prefetch=1,
            grid=(pairs,),
            in_specs=[spec(0), spec(1), spec(0), spec(1)] + [pl.BlockSpec(memory_space=pl.ANY)] * len(waits),
            out_specs=[ends, ends],
        ),
        out_shape=[
            jax.ShapeDtypeStruct((pairs, rows, columns), F32),
            jax.ShapeDtypeStruct((pairs, rows, columns), kind),
        ],
        compiler_params=pltpu.CompilerParams(vmem_limit_bytes=VMEM_BYTES),
        cost_estimate=pl.CostEstimate(flops=1, bytes_accessed=1, transcendentals=0),
        name="combine",
    )(bit, keep, keep, arrived, arrived, *in_hbm(waits))


def partner(values, distance):
    return lax.ppermute(values, "tensor", [(i, i ^ distance) for i in range(4)])


def together(*values):
    return lax.optimization_barrier(values)


def dp_paired():
    return lax.axis_size("dp") % 2 == 0


def half_of(own, shared):
    odd = lax.axis_index("dp") & 1
    return lax.dynamic_slice_in_dim(own, odd * (shared // 2), shared // 2, 0)


def swapped(mine, rest):
    odd = (lax.axis_index("dp") & 1) == 1
    other = lax.ppermute(mine, "dp", [(i, i ^ 1) for i in range(lax.axis_size("dp"))])
    return jnp.concatenate([jnp.where(odd, other, mine), jnp.where(odd, mine, other)] + rest, axis=0)


def straight(pieces, index):
    odd = (index & 1) == 1
    upper = (index & 2) == 2
    low = [jnp.where(odd, pieces[k ^ 1], pieces[k]) for k in range(4)]
    return [jnp.where(upper, low[k ^ 2], low[k]) for k in range(4)]


def rows_to_batches(first, inputs, cotangent, index):
    pieces = []
    for k in range(4):
        both = [lax.dynamic_index_in_dim(v, index ^ k, 0, keepdims=False) for v in (inputs, cotangent)]
        pieces.append(jnp.where(first, both[0], both[1]))
    pieces = [pieces[0]] + [partner(pieces[k], k) for k in range(1, 4)]
    return jnp.concatenate(straight(pieces, index), axis=0)


def rows_sent(rows, index):
    own = rows.shape[0] // 4
    pieces = [lax.dynamic_slice_in_dim(rows, (index ^ k) * own, own, 0) for k in range(4)]
    return [pieces[0]] + [partner(pieces[k], k) for k in range(1, 4)]


def dp_stages():
    count = lax.axis_size("dp")
    return [1 << i for i in range(count.bit_length() - 1)] if count & (count - 1) == 0 else None


class Reduction:
    def __init__(self, keep, arriving, kind):
        self.keep, self.arriving, self.kind = keep, arriving, kind
        self.share = keep.shape[0] // lax.axis_size("dp")
        self.left = dp_stages()

    def begin(self, *waits):
        distance = self.left.pop(0)
        columns = self.keep.shape[-1]
        bit = (lax.axis_index("dp") // distance) & 1
        shape = (self.keep.size // (2 * columns * self.share), 2, self.share, columns)
        self.keep, sent = combine(
            self.keep.reshape(shape), self.arriving.reshape(shape), bit[None], self.kind, waits
        )
        total = lax.axis_size("dp")
        self.arriving = lax.ppermute(sent, "dp", [(i, i ^ distance) for i in range(total)])
        return sent

    def result(self, *waits):
        if self.left is None:
            whole = (self.keep + self.arriving.astype(F32)).astype(self.kind)
            return lax.psum_scatter(whole, "dp", scatter_dimension=0, tiled=True).astype(F32)
        while self.left:
            self.begin(*waits)
        whole = self.keep + self.arriving.astype(F32)
        return whole.reshape(whole.shape[-2:])


def body(
    inputs,
    cotangent,
    seq_lengths,
    w_attn,
    b_qv,
    w_proj,
    b_proj,
    w_fc,
    b_fc,
    w_out,
    b_out,
    ln_gain,
    ln_bias,
):
    micro, own, model = inputs.shape
    total = own * lax.axis_size("tensor")
    width = w_attn.shape[-1]
    groups = lax.axis_size("dp")
    me = lax.axis_index("tensor")
    first = lax.axis_index("section") == 0

    units = w_fc.shape[-1]
    shared = units // 3 if units % 96 == 0 else units
    unit_attn = jnp.concatenate([w_attn[0].reshape(model, 3 * width), w_proj[0].T], axis=1)
    paired = dp_paired()
    first_sent = half_of(unit_attn, model) if paired else unit_attn
    attn_far = partner(first_sent, 2)
    staged = rows_to_batches(first, inputs, cotangent, me)
    split_own = jnp.concatenate([b_qv[0, 0], jnp.zeros_like(b_qv[0, 0]), b_qv[0, 1], b_fc[0]])
    split_far = partner(split_own, 2)
    split_all = [split_own, partner(split_own, 1), split_far, partner(split_far, 1)]
    b_mixed = [v[None, None, : 3 * width].astype(F32) for v in split_all]
    b_fcs = [v[None, None, 3 * width :].astype(F32) for v in split_all]
    b_proj = b_proj.astype(F32)
    b_out = b_out.astype(F32)
    ln_gain = ln_gain[0].astype(F32)
    ln_bias = ln_bias[0].astype(F32)
    norm_one = (ln_gain[0:1], ln_bias[0:1], b_proj)
    norm_two = (ln_gain[1:2], ln_bias[1:2])

    lengths = lax.dynamic_index_in_dim(seq_lengths[0], me, 0, keepdims=False)
    ends = jnp.cumsum(lengths)
    position = jnp.arange(total, dtype=jnp.int32)
    segment = jnp.sum((position[:, None] >= ends[None, :]).astype(jnp.int32), axis=1)
    live = (position < ends[-1]).astype(F32)[:, None]
    last = (live, b_out)

    def attend_one(middle, k, normed, cost=1):
        return attend(middle, segment, attn[k][None], b_mixed[k], normed=normed, cost=cost)[0]

    def feed_one(result, k, normed, ending=None, cost=1):
        return feed(result, fc[k][None], out[k][None], b_fcs[k], normed=normed, last=ending, cost=cost)[0]

    attn = {0: unit_attn, 1: partner(unit_attn, 1)}
    fc = {0: w_fc[0], 1: partner(w_fc[0], 1)}
    out = {0: w_out[0], 1: partner(w_out[0], 1)}
    fc_far = partner(half_of(w_fc[0], model) if paired else w_fc[0], 2)
    middle, normed = attend(
        staged, segment, attn[0][None], b_mixed[0], first=norm_one, waits=split_all[2:], cost=MID
    )[:2]
    if paired:
        out_sent, rest, middle = together(half_of(w_out[0], shared), w_out[0, shared:], middle)
        out_far, rest = partner(out_sent, 2), [partner(rest, 2)] if shared < units else []
        attn_far, middle = together(attn_far, middle)
        attn_far = swapped(attn_far, [])
        fc_far, middle = together(fc_far, middle)
        fc_far = swapped(fc_far, [])
    else:
        out_sent, middle = together(w_out[0], middle)
        out_far = partner(out_sent, 2)
    middle = attend_one(middle, 1, normed, MID)
    if paired:
        out_far, middle = together(out_far, middle)
        out_far = swapped(out_far, rest)
    attn[2], attn[3] = attn_far, partner(attn_far, 1)
    middle = attend_one(middle, 2, normed, MID)
    middle = attend_one(middle, 3, normed, MID)
    fc_far, middle = together(fc_far, middle)
    result, normed = feed(middle, fc[0][None], out[0][None], b_fcs[0], first=norm_two, cost=MID)
    out_far, result = together(out_far, result)
    result = feed_one(result, 1, normed, cost=MID)
    fc[2], fc[3] = fc_far, partner(fc_far, 1)
    out[2], out[3] = out_far, partner(out_far, 1)
    result = feed_one(result, 2, normed)
    result = feed_one(result, 3, normed, last)
    received = lax.ppermute(result, "section", [(0, 1)])

    attn, fc, out, result = together(*[[v[k] for k in PLACES] for v in (attn, fc, out)], result)
    attn, fc, out = [jnp.stack(v) for v in (attn, fc, out)]
    b_mixed, b_fcs = [jnp.concatenate([v[k] for k in PLACES]) for v in (b_mixed, b_fcs)]
    rows = jnp.where(first, staged, received)
    middle, normed, mixed, context, logsum = attend(rows, segment, attn, b_mixed, first=norm_one, cost=LONG)
    result, normed_two, slope, active, *active_away = feed(
        middle, fc, out, b_fcs, first=norm_two, last=last, keep=True, cost=LONG
    )
    section_out = rows_sent(result, me)
    normed_other = partner(normed, 1)
    normed_two_other = partner(normed_two, 1)
    active_other = [partner(v, 1) for v in active_away]

    fed = feed_back(staged, live, middle, slope, fc, out, norm_two[0], cost=LONG)
    early = (normed_other, normed_two_other, *active_other)
    passed = attend_back(fed[1], fed[0], rows, segment, attn, mixed, context, logsum, norm_one[0], fed[-1], fed[-2], early, LONG)
    coming = lax.ppermute(passed[0], "section", [(1, 0)])
    coming, *section_out = together(coming, *section_out)
    grad_out = jnp.where(first, coming, staged)

    branch = (live * grad_out.astype(F32)).astype(BF16)
    ((keep_out, send_out),) = outer((branch, [partner(branch, 1)], active, active_other))
    sum_out = Reduction(keep_out, partner(send_out, 2), BF16)
    middle_grad, grad_attn, attn_high, attn_low, branch, hid, *hid_away, g_bfc, small_two = feed_back(
        grad_out, live, middle, slope, fc, out, norm_two[0], (send_out,), 1, True
    )
    hid_other = [partner(v, 1) for v in hid_away]
    grad_attn_other = [partner(attn_high, 1), partner(attn_low, 1)]
    ((keep_fc, send_fc),) = outer((normed_two, [normed_two_other], hid, hid_other))
    sum_fc = Reduction(keep_fc, partner(send_fc, 2), BF16)
    grad_rows, mix, *mix_away, pack = attend_back(
        grad_attn, middle_grad, rows, segment, attn, mixed, context, logsum, norm_one[0], small_two, g_bfc, (send_fc,)
    )
    staggered = sum_out.left is not None
    if staggered:
        token = sum_out.begin(grad_rows)
        *mix_away, pack, token = together(*mix_away, pack, token)
    pack_other = partner(pack, 1)
    mix_other = [partner(v, 1) for v in mix_away]
    kept = outer(
        (normed, [normed_other], mix, mix_other),
        (grad_attn, grad_attn_other, context, mix_other),
        chunks=2,
        packs=(pack, pack_other),
        waits=(mix_away[0],),
    )
    kept = [[v.reshape(-1, v.shape[-1]) for v in pair] for pair in kept]
    sums_attn = [Reduction(keep, partner(send, 2), BF16) for keep, send in kept]
    if staggered:
        token = sum_out.begin(kept[0][1])
        token = sum_fc.begin(token)
        token = sums_attn[0].begin(token)
        grad_rows, token = together(grad_rows, token)
        input_grad = rows_sent(grad_rows, me)
        token = sum_fc.begin(token)
        token = sums_attn[1].begin(token)
        g_fc = sum_fc.result()
        token = sums_attn[0].begin(token, g_fc)
        token = sums_attn[1].begin(token)
        *input_grad, token = together(*input_grad, token)
        *section_out, token = together(*section_out, token)
    else:
        input_grad = rows_sent(grad_rows, me)
        g_fc = sum_fc.result()
    section_out, input_grad = [jnp.stack(straight(v, me)) for v in (section_out, input_grad)]
    g_out = sum_out.result()
    g_attn = [v.result() for v in sums_attn]
    g_attn = jnp.concatenate(g_attn, axis=1)

    g_attn, sums = g_attn[:-16], g_attn[-16:]
    g_wattn = g_attn[:, : 3 * width].reshape(-1, 3, width)
    g_wproj = g_attn[:, 3 * width :].T
    g_wout = g_out.T

    share = model // (groups * 4)
    g_bqv = sums[6, : 2 * width].reshape(2, width)
    g_bfc = sums[7]
    sums = lax.dynamic_slice_in_dim(sums, (lax.axis_index("dp") * 4 + me) * share, share, 1)
    return (
        section_out[None],
        input_grad[None],
        g_wattn[None],
        g_bqv[None],
        g_wproj[None],
        sums[4][None],
        g_fc[None],
        g_bfc[None],
        g_wout[None],
        sums[5][None],
        jnp.stack([sums[0], sums[2]])[None],
        jnp.stack([sums[1], sums[3]])[None],
    )


def solution(mesh):
    in_specs = (
        P(None, ("dp", "tensor"), None),
        P(None, ("dp", "tensor"), None),
        P("dp", None, None),
        P("section", None, None, "tensor"),
        P("section", None, "tensor"),
        P("section", "tensor", None),
        P("section", None),
        P("section", None, "tensor"),
        P("section", "tensor"),
        P("section", "tensor", None),
        P("section", None),
        P("section", None, None),
        P("section", None, None),
    )
    out_specs = (
        P("section", None, ("dp", "tensor"), None),
        P("section", None, ("dp", "tensor"), None),
        P("section", "dp", None, "tensor"),
        P("section", None, "tensor"),
        P("section", "tensor", "dp"),
        P("section", ("dp", "tensor")),
        P("section", "dp", "tensor"),
        P("section", "tensor"),
        P("section", "tensor", "dp"),
        P("section", ("dp", "tensor")),
        P("section", None, ("dp", "tensor")),
        P("section", None, ("dp", "tensor")),
    )
    return jax.shard_map(body, mesh=mesh, in_specs=in_specs, out_specs=out_specs, check_vma=False)
```

```python
import functools

import jax
import jax.numpy as jnp
from jax import lax
from jax.experimental import pallas as pl
from jax.experimental.pallas import tpu as pltpu
from jax.sharding import PartitionSpec as P

HEAD_DIM = 64
SCALE = HEAD_DIM**-0.5
F32 = jnp.float32
BF16 = jnp.bfloat16
PLACES = (0, 2, 1, 3)
GELU_A = (2.0 / jnp.pi) ** 0.5
GELU_B = 0.044715
VMEM_BYTES = 24 * 2**20
LONG = 10**10
MID = 1


def dot(left, right, dims):
    return lax.dot_general(left, right, (dims, ((), ())), preferred_element_type=F32)


NN = ((1,), (0,))
NT = ((1,), (1,))
TN = ((0,), (0,))


def normalized(rows):
    center = jnp.mean(rows, axis=-1, keepdims=True)
    centred = rows - center
    spread = lax.rsqrt(jnp.mean(centred * centred, axis=-1, keepdims=True) + 1e-05)
    return centred * spread, spread


def norm_back(rows, gain, grad):
    unit, spread = normalized(rows)
    scaled = grad * gain
    inner = jnp.mean(scaled * unit, axis=-1, keepdims=True)
    back = spread * (scaled - jnp.mean(scaled, axis=-1, keepdims=True) - unit * inner)
    return back, col_sum(grad * unit), col_sum(grad)


def col_sum(values):
    return jnp.sum(values, axis=0, keepdims=True)


def fill_mask(seg_col, seg_row, mask):
    total = mask.shape[0]
    key = lax.broadcasted_iota(jnp.int32, (total, total), 0)
    query = lax.broadcasted_iota(jnp.int32, (total, total), 1)
    allowed = (seg_col[...] == seg_row[...]) & (key <= query)
    mask[...] = jnp.where(allowed, 0.0, -1e30)


def bands(total):
    span = total // 2 if total % 256 == 0 else total
    return [(start, start + span) for start in range(0, total, span)]


def share_out(step, values, near, far):
    if near is not None:

        @pl.when(step < 2)
        def keep_near():
            near[0] = values

    for index, refs in enumerate(far):

        @pl.when(step == 2 + index)
        def keep_far(refs=refs):
            rows = values.shape[0] // len(refs)
            for part, ref in enumerate(refs):
                ref[...] = values[part * rows : (part + 1) * rows]


def attend_kernel(fresh, rows, seg_col, seg_row, weight, bias, *rest):
    if fresh:
        gain, shift, b_proj, total_out, normed_out, mixed_out, context_out, logsum_out, mask, total = rest
        normed = normed_out
    else:
        normed, total_out, mixed_out, context_out, logsum_out, mask, total = rest
    step = pl.program_id(0)
    width = context_out.shape[-1]
    count = rows.shape[0]

    @pl.when(step == 0)
    def start():
        fill_mask(seg_col, seg_row, mask)
        here = rows[...].astype(F32)
        if fresh:
            unit, unused = normalized(here)
            normed_out[...] = (unit * gain[...] + shift[...]).astype(BF16)
            total[...] = here + b_proj[...]
        else:
            total[...] = here

    wide = weight[0]
    mixed = (dot(normed[...], wide[:, : 3 * width], NN) + bias[0]).astype(BF16)
    mixed_out[0] = mixed
    pieces, stats = [], []
    for head in range(width // HEAD_DIM):
        at = head * HEAD_DIM
        queries = mixed[:, at : at + HEAD_DIM] * SCALE
        keys = mixed[:, width + at : width + at + HEAD_DIM]
        values = mixed[:, 2 * width + at : 2 * width + at + HEAD_DIM]
        made, logs = [], []
        for low, high in bands(count):
            scores = dot(keys[:high], queries[low:high], NT) + mask[:high, low:high]
            top = jnp.max(scores, axis=0, keepdims=True)
            expo = jnp.exp(scores - top)
            norm = jnp.sum(expo, axis=0, keepdims=True)
            made.append(dot(values[:high], expo.astype(BF16), TN) * (1.0 / norm))
            logs.append(top + jnp.log(norm))
        pieces.append(jnp.concatenate(made, axis=1))
        stats.append(jnp.concatenate(logs, axis=1))
    context = jnp.concatenate(pieces, axis=0).T.astype(BF16)
    context_out[0] = context
    stats.append(jnp.zeros((8 - len(stats), count), F32))
    logsum_out[0] = jnp.concatenate(stats, axis=0)
    total[...] += dot(context, wide[:, 3 * width :], NT)

    @pl.when(step == pl.num_programs(0) - 1)
    def finish():
        total_out[...] = total[...]


def feed_kernel(fresh, last, keep, rows, fc, out, b_fc, *rest):
    rest = list(rest)
    if fresh:
        gain, shift = rest[:2]
        rest = rest[2:]
    else:
        normed = rest.pop(0)
    if last:
        live, b_out = rest[:2]
        rest = rest[2:]
    result = rest.pop(0)
    if fresh:
        normed = rest.pop(0)
    if keep:
        slope_out, active_near, active_far = rest[0], rest[1], (rest[2:3], rest[3:4])
    total = rest[-1]
    step = pl.program_id(0)
    count = rows.shape[0]

    @pl.when(step == 0)
    def start():
        if fresh:
            unit, unused = normalized(rows[...])
            normed[...] = (unit * gain[...] + shift[...]).astype(BF16)
        total[...] = rows[...]

    made = []
    for low, high in bands(count):
        hidden = dot(normed[low:high, :], fc[0], NN) + b_fc[0]
        square = hidden * hidden
        tanh = jnp.tanh(GELU_A * hidden * (1.0 + GELU_B * square))
        upper = 0.5 * (1.0 + tanh)
        active = (hidden * upper).astype(BF16)
        total[low:high, :] += dot(active, out[0], NN)
        if keep:
            inner = GELU_A * hidden * (1.0 + 3.0 * GELU_B * square)
            slope_out[0, low:high, :] = (upper + upper * (1.0 - tanh) * inner).astype(BF16)
            made.append(active)
    if keep:
        share_out(step, jnp.concatenate(made, axis=0), active_near, active_far)

    @pl.when(step == pl.num_programs(0) - 1)
    def finish():
        if last:
            result[...] = (live[...] * (total[...] + b_out[...])).astype(BF16)
        else:
            result[...] = total[...]


def feed_back_kernel(
    grad, live, middle, slope, fc, out, gain, grad_middle, grad_attn, attn_high, attn_low, branch_out, near,
    far_one, far_one_low, far_two, far_two_low, b_fc_out, small, total,
):
    step = pl.program_id(0)
    count = grad.shape[0]

    @pl.when(step == 0)
    def start():
        branch_out[...] = (live[...] * grad[...].astype(F32)).astype(BF16)
        total[...] = jnp.zeros_like(total)

    bias_sum = 0.0
    made = []
    for low, high in bands(count):
        grad_active = dot(branch_out[low:high, :], out[0], NT)
        grad_hidden = (grad_active * slope[0, low:high, :].astype(F32)).astype(BF16)
        bias_sum = bias_sum + col_sum(grad_hidden.astype(F32))
        total[low:high, :] += dot(grad_hidden, fc[0], NT)
        made.append(grad_hidden)
    b_fc_out[0] = bias_sum
    share_out(step, jnp.concatenate(made, axis=0), near, ((far_one, far_one_low), (far_two, far_two_low)))

    @pl.when(step == pl.num_programs(0) - 1)
    def finish():
        back, gain_sum, shift_sum = norm_back(middle[...], gain[...], total[...])
        back = back + live[...] * grad[...].astype(F32)
        grad_middle[...] = back
        rounded = back.astype(BF16)
        grad_attn[...] = rounded
        attn_high[...] = rounded[: count // 2]
        attn_low[...] = rounded[count // 2 :]
        sums = [gain_sum, shift_sum, col_sum(rounded.astype(F32)), col_sum(branch_out[...].astype(F32))]
        small[...] = jnp.concatenate(sums + [jnp.zeros((4, gain_sum.shape[1]), F32)], axis=0)


def attend_back_kernel(
    grad_attn, grad_middle, rows, seg_col, seg_row, weight, mixed, context, logsum, gain, small_two, b_fc,
    grad_rows, near, far_one, far_one_low, far_two, far_two_low, pack, mask, total,
):
    step = pl.program_id(0)
    width = context.shape[-1]
    count = grad_attn.shape[0]

    @pl.when(step == 0)
    def start():
        fill_mask(seg_col, seg_row, mask)
        total[...] = jnp.zeros_like(total)

    wide = weight[0]
    grad_context = dot(grad_attn[...], wide[:, 3 * width :], NN).astype(BF16)
    product = (grad_context.astype(F32) * context[0].astype(F32)).T
    every = mixed[0]
    all_q, all_k, all_v = [], [], []
    for head in range(width // HEAD_DIM):
        at = head * HEAD_DIM
        queries = every[:, at : at + HEAD_DIM] * SCALE
        keys = every[:, width + at : width + at + HEAD_DIM]
        values = every[:, 2 * width + at : 2 * width + at + HEAD_DIM]
        grad = grad_context[:, at : at + HEAD_DIM]
        weighted = col_sum(product[at : at + HEAD_DIM, :])
        grad_q, grad_k, grad_v = [], [], []
        for low, high in bands(count):
            scores = dot(keys[:high], queries[low:high], NT) + mask[:high, low:high]
            probs = jnp.exp(scores - logsum[0, head : head + 1, low:high])
            grad_probs = dot(values[:high], grad[low:high], NT)
            grad_scores = (probs * (grad_probs - weighted[:, low:high])).astype(BF16)
            grad_v.append(dot(probs.astype(BF16), grad[low:high], NN))
            grad_k.append(dot(grad_scores, queries[low:high], NN))
            grad_q.append(dot(keys[:high], grad_scores, TN) * SCALE)
        for parts, whole in ((grad_k, all_k), (grad_v, all_v)):
            summed = parts[-1]
            for part in parts[:-1]:
                reach = part.shape[0]
                summed = jnp.concatenate([summed[:reach] + part, summed[reach:]], axis=0)
            whole.append(summed)
        all_q.append(jnp.concatenate(grad_q, axis=1))
    first = jnp.concatenate(all_q, axis=0).T
    grad_mixed = jnp.concatenate([first] + all_k + all_v, axis=1).astype(BF16)

    share_out(step, grad_mixed, near, ())
    both = jnp.concatenate([grad_mixed, context[0]], axis=1)
    share_out(step, both, None, ((far_one, far_one_low), (far_two, far_two_low)))
    sums = col_sum(grad_mixed.astype(F32))
    spare = jnp.zeros((1, pack.shape[-1] - 2 * width), F32)
    pack[pl.ds(8 + step, 1), :] = jnp.concatenate([sums[:, :width], sums[:, 2 * width :], spare], axis=1)
    total[...] += dot(grad_mixed, wide[:, : 3 * width], NT)

    @pl.when(step == pl.num_programs(0) - 1)
    def finish():
        back, gain_sum, shift_sum = norm_back(rows[...].astype(F32), gain[...], total[...])
        grad_rows[...] = (grad_middle[...] + back).astype(BF16)
        spare = jnp.zeros((2, gain_sum.shape[1]), F32)
        pack[:8, :] = jnp.concatenate([gain_sum, shift_sum, small_two[:4, :], spare], axis=0)
        pack[12:, :] = jnp.concatenate([b_fc[place] for place in range(4)], axis=0)


def joined(refs):
    values = [ref[...] for ref in refs]
    return jnp.concatenate(values, axis=0) if len(values) > 1 else values[0]


def outer_kernel(pairs, chunks, spans, halves, extra, *refs):
    ends = [sum(2 + span + 2 * halves for span in spans[:index]) for index in range(pairs + 1)]
    outs = refs[ends[-1] + 2 * extra :]
    for place in range(2):
        sums, taken = [], 0
        for index in range(pairs):
            left, *left_other = refs[ends[index] : ends[index] + 1 + spans[index]]
            right, *others = refs[ends[index] + 1 + spans[index] : ends[index + 1]]
            left_other = joined(left_other)
            columns = right.shape[-1]
            away = joined(others[place * halves : (place + 1) * halves])[:, taken : taken + columns]
            taken += columns
            sums.append(dot(left[...], right[place], TN) + dot(left_other, away, TN))
        whole = sums[0] if pairs == 1 else jnp.concatenate(sums, axis=1)
        columns = whole.shape[1] // chunks
        for index in range(chunks):
            part = whole[:, index * columns : (index + 1) * columns]
            kind = BF16 if place else F32
            result = outs[2 * index + place]
            if not extra:
                result[...] = part.astype(kind)
                continue
            pack, pack_other = refs[ends[-1] : ends[-1] + 2]
            at = slice(index * columns, (index + 1) * columns)
            lines = [pack[:6, at] + pack_other[:6, at]]
            for first in (8 + place, 12 + place):
                lines.append(pack[first : first + 1, at] + pack_other[first + 2 : first + 3, at])
            lines.append(jnp.zeros((8, columns), F32))
            lines = jnp.concatenate(lines, axis=0).astype(kind)
            share = part.shape[0] // result.shape[0]
            for dest in range(result.shape[0]):
                result[dest, :share, :] = part[dest * share : (dest + 1) * share].astype(kind)
                result[dest, share:, :] = lines


def combine_kernel(bit, keep, keep_other, arrived, arrived_other, kept, sent):
    kept[0] = keep[0, 0] + arrived[0, 0].astype(F32)
    sent[0] = (keep_other[0, 0] + arrived_other[0, 0].astype(F32)).astype(sent.dtype)


def block(shape):
    return pl.BlockSpec(shape, lambda step: (0,) * len(shape))


def first_two(shape):
    return pl.BlockSpec((2,) + shape[1:], lambda step: (0, 0, 0))


def stepped(shape):
    return pl.BlockSpec((1,) + shape[1:], lambda step: (step,) + (0,) * (len(shape) - 1))


def near_spec(shape):
    return pl.BlockSpec((1,) + shape[1:], lambda step: (jnp.minimum(step, 1), 0, 0))


def in_hbm(values):
    return [pltpu.with_memory_space_constraint(v, pltpu.HBM) if v.size > 2**17 else v for v in values]


def call(kernel, name, steps, ins, outs, scratch, waits=(), cost=1, stay=False):
    count = len(ins)
    skip = count + len(waits)
    values = [value for value, kind in ins]
    if stay:
        values = in_hbm(values)

    def run(*refs):
        kernel(*refs[:count], *refs[skip:])

    return pl.pallas_call(
        run,
        grid=(steps,),
        in_specs=[kind(value.shape) for value, kind in ins] + [pl.BlockSpec(memory_space=pl.ANY)] * len(waits),
        out_specs=[kind(shape) for shape, dtype, kind in outs],
        out_shape=[jax.ShapeDtypeStruct(shape, dtype) for shape, dtype, kind in outs],
        scratch_shapes=scratch,
        compiler_params=pltpu.CompilerParams(vmem_limit_bytes=VMEM_BYTES),
        cost_estimate=pl.CostEstimate(flops=cost, bytes_accessed=cost, transcendentals=0),
        name=name,
    )(*values, *in_hbm(waits))


def attend(rows, segment, weight, bias, normed=None, first=None, waits=(), cost=1):
    steps = weight.shape[0]
    total, model = rows.shape
    width = bias.shape[-1] // 3
    ins = [(rows, block), (segment[:, None], block), (segment[None, :], block), (weight, stepped), (bias, stepped)]
    outs = [((total, model), F32, block)]
    if first is None:
        ins.append((normed, block))
    else:
        ins += [(v, block) for v in first]
        outs.append(((total, model), BF16, block))
    outs += [
        ((steps, total, 3 * width), BF16, stepped),
        ((steps, total, width), BF16, stepped),
        ((steps, 8, total), F32, stepped),
    ]
    return call(
        functools.partial(attend_kernel, first is not None), "attend", steps, ins, outs,
        [pltpu.VMEM((total, total), F32), pltpu.VMEM((total, model), F32)], waits, cost,
    )


def feed(rows, fc, out, b_fc, normed=None, first=None, last=None, keep=False, cost=1):
    steps = fc.shape[0]
    total, model = rows.shape
    units = fc.shape[-1]
    ins = [(rows, block), (fc, stepped), (out, stepped), (b_fc, stepped)]
    outs = [((total, model), F32 if last is None else BF16, block)]
    if first is None:
        ins.append((normed, block))
    else:
        ins += [(v, block) for v in first]
        outs.append(((total, model), BF16, block))
    if last is not None:
        ins += [(v, block) for v in last]
    if keep:
        outs += [
            ((steps, total, units), BF16, stepped),
            ((steps // 2, total, units), BF16, near_spec),
            ((total, units), BF16, block),
            ((total, units), BF16, block),
        ]
    return call(
        functools.partial(feed_kernel, first is not None, last is not None, keep), "feed", steps, ins, outs,
        [pltpu.VMEM((total, model), F32)], (), cost,
    )


def feed_back(grad, live, middle, slope, fc, out, gain, waits=(), cost=1, stay=False):
    steps = fc.shape[0]
    total, model = grad.shape
    units = fc.shape[-1]
    if stay:
        slope, fc, out = in_hbm((slope, fc, out))
    ins = [(grad, block), (live, block), (middle, block), (slope, stepped), (fc, stepped), (out, stepped), (gain, block)]
    outs = [
        ((total, model), F32, block),
        ((total, model), BF16, block),
        *[((total // 2, model), BF16, block)] * 2,
        ((total, model), BF16, block),
        ((steps // 2, total, units), BF16, near_spec),
        *[((total // 2, units), BF16, block)] * 4,
        ((steps, 1, units), F32, stepped),
        ((8, model), F32, block),
    ]
    return call(
        feed_back_kernel, "feed_back", steps, ins, outs, [pltpu.VMEM((total, model), F32)], waits, cost
    )


def attend_back(grad_attn, grad_middle, rows, segment, weight, mixed, context, logsum, gain, small_two, b_fc, waits=(), cost=1):
    steps = weight.shape[0]
    total, model = grad_attn.shape
    width = context.shape[-1]
    ins = [
        (grad_attn, block), (grad_middle, block), (rows, block), (segment[:, None], block), (segment[None, :], block),
        (weight, stepped), (mixed, stepped), (context, stepped), (logsum, stepped), (gain, block),
        (small_two, block), (b_fc, block),
    ]
    outs = [
        ((total, model), BF16, block),
        ((steps // 2, total, 3 * width), BF16, near_spec),
        *[((total // 2, 4 * width), BF16, block)] * 4,
        ((16, model), F32, block),
    ]
    return call(
        attend_back_kernel, "attend_back", steps, ins, outs,
        [pltpu.VMEM((total, total), F32), pltpu.VMEM((total, model), F32)], waits, cost,
    )


def outer(*pairs, chunks=1, packs=(), waits=()):
    ins, columns, spans = [], 0, []
    for left, left_other, right, others in pairs:
        ins += [(v, block) for v in (left, *left_other)] + [(right, first_two)] + [(v, block) for v in others]
        spans.append(len(left_other))
        halves = len(others) // 2
        columns += right.shape[-1]
    model = pairs[0][0].shape[1]
    groups = lax.axis_size("dp")
    shape = (groups, model // groups + 16, columns // chunks) if packs else (model, columns // chunks)
    outs = [(shape, F32, block), (shape, BF16, block)] * chunks
    ins += [(v, block) for v in packs]
    made = call(functools.partial(outer_kernel, len(pairs), chunks, spans, halves, bool(packs)), "outer", 1, ins, outs, [], waits, 1, True)
    return [list(made[2 * index : 2 * index + 2]) for index in range(chunks)]


def combine(keep, arrived, bit, kind, waits=()):
    pairs, unused, rows, columns = keep.shape

    def run(*refs):
        combine_kernel(*refs[:5], *refs[5 + len(waits) :])

    def spec(flip):
        return pl.BlockSpec((1, 1, rows, columns), lambda step, where: (step, flip + (1 - 2 * flip) * where[0], 0, 0))

    ends = pl.BlockSpec((1, rows, columns), lambda step, where: (step, 0, 0))
    return pl.pallas_call(
        run,
        grid_spec=pltpu.PrefetchScalarGridSpec(
            num_scalar_prefetch=1,
            grid=(pairs,),
            in_specs=[spec(0), spec(1), spec(0), spec(1)] + [pl.BlockSpec(memory_space=pl.ANY)] * len(waits),
            out_specs=[ends, ends],
        ),
        out_shape=[
            jax.ShapeDtypeStruct((pairs, rows, columns), F32),
            jax.ShapeDtypeStruct((pairs, rows, columns), kind),
        ],
        compiler_params=pltpu.CompilerParams(vmem_limit_bytes=VMEM_BYTES),
        cost_estimate=pl.CostEstimate(flops=1, bytes_accessed=1, transcendentals=0),
        name="combine",
    )(bit, keep, keep, arrived, arrived, *in_hbm(waits))


def partner(values, distance):
    return lax.ppermute(values, "tensor", [(i, i ^ distance) for i in range(4)])


def together(*values):
    return lax.optimization_barrier(values)


def dp_paired():
    return lax.axis_size("dp") % 2 == 0


def half_of(own, shared):
    odd = lax.axis_index("dp") & 1
    return lax.dynamic_slice_in_dim(own, odd * (shared // 2), shared // 2, 0)


def swapped(mine, rest):
    odd = (lax.axis_index("dp") & 1) == 1
    other = lax.ppermute(mine, "dp", [(i, i ^ 1) for i in range(lax.axis_size("dp"))])
    return jnp.concatenate([jnp.where(odd, other, mine), jnp.where(odd, mine, other)] + rest, axis=0)


def straight(pieces, index):
    odd = (index & 1) == 1
    upper = (index & 2) == 2
    low = [jnp.where(odd, pieces[k ^ 1], pieces[k]) for k in range(4)]
    return [jnp.where(upper, low[k ^ 2], low[k]) for k in range(4)]


def rows_to_batches(first, inputs, cotangent, index):
    pieces = []
    for k in range(4):
        both = [lax.dynamic_index_in_dim(v, index ^ k, 0, keepdims=False) for v in (inputs, cotangent)]
        pieces.append(jnp.where(first, both[0], both[1]))
    pieces = [pieces[0]] + [partner(pieces[k], k) for k in range(1, 4)]
    return jnp.concatenate(straight(pieces, index), axis=0)


def rows_sent(rows, index):
    own = rows.shape[0] // 4
    pieces = [lax.dynamic_slice_in_dim(rows, (index ^ k) * own, own, 0) for k in range(4)]
    return [pieces[0]] + [partner(pieces[k], k) for k in range(1, 4)]


def dp_stages():
    count = lax.axis_size("dp")
    return [1 << i for i in range(count.bit_length() - 1)] if count & (count - 1) == 0 else None


class Reduction:
    def __init__(self, keep, arriving, kind):
        self.keep, self.arriving, self.kind = keep, arriving, kind
        self.share = keep.shape[0] // lax.axis_size("dp")
        self.left = dp_stages()

    def begin(self, *waits):
        distance = self.left.pop(0)
        columns = self.keep.shape[-1]
        bit = (lax.axis_index("dp") // distance) & 1
        shape = (self.keep.size // (2 * columns * self.share), 2, self.share, columns)
        self.keep, sent = combine(
            self.keep.reshape(shape), self.arriving.reshape(shape), bit[None], self.kind, waits
        )
        total = lax.axis_size("dp")
        self.arriving = lax.ppermute(sent, "dp", [(i, i ^ distance) for i in range(total)])
        return sent

    def result(self, *waits):
        if self.left is None:
            whole = (self.keep + self.arriving.astype(F32)).astype(self.kind)
            return lax.psum_scatter(whole, "dp", scatter_dimension=0, tiled=True).astype(F32)
        while self.left:
            self.begin(*waits)
        whole = self.keep + self.arriving.astype(F32)
        return whole.reshape(whole.shape[-2:])


def body(
    inputs,
    cotangent,
    seq_lengths,
    w_attn,
    b_qv,
    w_proj,
    b_proj,
    w_fc,
    b_fc,
    w_out,
    b_out,
    ln_gain,
    ln_bias,
):
    micro, own, model = inputs.shape
    total = own * lax.axis_size("tensor")
    width = w_attn.shape[-1]
    groups = lax.axis_size("dp")
    me = lax.axis_index("tensor")
    first = lax.axis_index("section") == 0

    units = w_fc.shape[-1]
    shared = units // 3 if units % 96 == 0 else units
    unit_attn = jnp.concatenate([w_attn[0].reshape(model, 3 * width), w_proj[0].T], axis=1)
    paired = dp_paired()
    first_sent = half_of(unit_attn, model) if paired else unit_attn
    attn_far = partner(first_sent, 2)
    staged = rows_to_batches(first, inputs, cotangent, me)
    split_own = jnp.concatenate([b_qv[0, 0], jnp.zeros_like(b_qv[0, 0]), b_qv[0, 1], b_fc[0]])
    split_far = partner(split_own, 2)
    split_all = [split_own, partner(split_own, 1), split_far, partner(split_far, 1)]
    b_mixed = [v[None, None, : 3 * width].astype(F32) for v in split_all]
    b_fcs = [v[None, None, 3 * width :].astype(F32) for v in split_all]
    b_proj = b_proj.astype(F32)
    b_out = b_out.astype(F32)
    ln_gain = ln_gain[0].astype(F32)
    ln_bias = ln_bias[0].astype(F32)
    norm_one = (ln_gain[0:1], ln_bias[0:1], b_proj)
    norm_two = (ln_gain[1:2], ln_bias[1:2])

    lengths = lax.dynamic_index_in_dim(seq_lengths[0], me, 0, keepdims=False)
    ends = jnp.cumsum(lengths)
    position = jnp.arange(total, dtype=jnp.int32)
    segment = jnp.sum((position[:, None] >= ends[None, :]).astype(jnp.int32), axis=1)
    live = (position < ends[-1]).astype(F32)[:, None]
    last = (live, b_out)

    def attend_one(middle, k, normed, cost=1):
        return attend(middle, segment, attn[k][None], b_mixed[k], normed=normed, cost=cost)[0]

    def feed_one(result, k, normed, ending=None, cost=1):
        return feed(result, fc[k][None], out[k][None], b_fcs[k], normed=normed, last=ending, cost=cost)[0]

    attn = {0: unit_attn, 1: partner(unit_attn, 1)}
    fc = {0: w_fc[0], 1: partner(w_fc[0], 1)}
    out = {0: w_out[0], 1: partner(w_out[0], 1)}
    fc_far = partner(half_of(w_fc[0], model) if paired else w_fc[0], 2)
    middle, normed = attend(
        staged, segment, attn[0][None], b_mixed[0], first=norm_one, waits=split_all[2:], cost=MID
    )[:2]
    if paired:
        out_sent, rest, middle = together(half_of(w_out[0], shared), w_out[0, shared:], middle)
        out_far, rest = partner(out_sent, 2), [partner(rest, 2)] if shared < units else []
        attn_far, middle = together(attn_far, middle)
        attn_far = swapped(attn_far, [])
        fc_far, middle = together(fc_far, middle)
        fc_far = swapped(fc_far, [])
    else:
        out_sent, middle = together(w_out[0], middle)
        out_far = partner(out_sent, 2)
    middle = attend_one(middle, 1, normed, MID)
    if paired:
        out_far, middle = together(out_far, middle)
        out_far = swapped(out_far, rest)
    attn[2], attn[3] = attn_far, partner(attn_far, 1)
    middle = attend_one(middle, 2, normed, MID)
    middle = attend_one(middle, 3, normed, MID)
    fc_far, middle = together(fc_far, middle)
    result, normed = feed(middle, fc[0][None], out[0][None], b_fcs[0], first=norm_two, cost=MID)
    out_far, result = together(out_far, result)
    result = feed_one(result, 1, normed, cost=MID)
    fc[2], fc[3] = fc_far, partner(fc_far, 1)
    out[2], out[3] = out_far, partner(out_far, 1)
    result = feed_one(result, 2, normed)
    result = feed_one(result, 3, normed, last)
    received = lax.ppermute(result, "section", [(0, 1)])

    attn, fc, out, result = together(*[[v[k] for k in PLACES] for v in (attn, fc, out)], result)
    attn, fc, out = [jnp.stack(v) for v in (attn, fc, out)]
    b_mixed, b_fcs = [jnp.concatenate([v[k] for k in PLACES]) for v in (b_mixed, b_fcs)]
    rows = jnp.where(first, staged, received)
    middle, normed, mixed, context, logsum = attend(rows, segment, attn, b_mixed, first=norm_one, cost=LONG)
    result, normed_two, slope, active, *active_away = feed(
        middle, fc, out, b_fcs, first=norm_two, last=last, keep=True, cost=LONG
    )
    section_out = rows_sent(result, me)
    normed_other = partner(normed, 1)
    normed_two_other = partner(normed_two, 1)
    active_other = [partner(v, 1) for v in active_away]

    fed = feed_back(staged, live, middle, slope, fc, out, norm_two[0], cost=LONG)
    early = (normed_other, normed_two_other, *active_other)
    passed = attend_back(fed[1], fed[0], rows, segment, attn, mixed, context, logsum, norm_one[0], fed[-1], fed[-2], early, LONG)
    coming = lax.ppermute(passed[0], "section", [(1, 0)])
    coming, *section_out = together(coming, *section_out)
    grad_out = jnp.where(first, coming, staged)

    branch = (live * grad_out.astype(F32)).astype(BF16)
    ((keep_out, send_out),) = outer((branch, [partner(branch, 1)], active, active_other))
    sum_out = Reduction(keep_out, partner(send_out, 2), BF16)
    middle_grad, grad_attn, attn_high, attn_low, branch, hid, *hid_away, g_bfc, small_two = feed_back(
        grad_out, live, middle, slope, fc, out, norm_two[0], (send_out,), 1, True
    )
    hid_other = [partner(v, 1) for v in hid_away]
    grad_attn_other = [partner(attn_high, 1), partner(attn_low, 1)]
    ((keep_fc, send_fc),) = outer((normed_two, [normed_two_other], hid, hid_other))
    sum_fc = Reduction(keep_fc, partner(send_fc, 2), BF16)
    grad_rows, mix, *mix_away, pack = attend_back(
        grad_attn, middle_grad, rows, segment, attn, mixed, context, logsum, norm_one[0], small_two, g_bfc, (send_fc,)
    )
    staggered = sum_out.left is not None
    if staggered:
        token = sum_out.begin(grad_rows)
        *mix_away, pack, token = together(*mix_away, pack, token)
    pack_other = partner(pack, 1)
    mix_other = [partner(v, 1) for v in mix_away]
    kept = outer(
        (normed, [normed_other], mix, mix_other),
        (grad_attn, grad_attn_other, context, mix_other),
        chunks=2,
        packs=(pack, pack_other),
        waits=(mix_away[0],),
    )
    kept = [[v.reshape(-1, v.shape[-1]) for v in pair] for pair in kept]
    sums_attn = [Reduction(keep, partner(send, 2), BF16) for keep, send in kept]
    if staggered:
        token = sum_out.begin(kept[0][1])
        token = sum_fc.begin(token)
        token = sums_attn[0].begin(token)
        grad_rows, token = together(grad_rows, token)
        input_grad = rows_sent(grad_rows, me)
        token = sums_attn[1].begin(token)
        token = sum_fc.begin(token)
        g_fc = sum_fc.result()
        token = sums_attn[0].begin(token, g_fc)
        token = sums_attn[1].begin(token)
        *input_grad, token = together(*input_grad, token)
        *section_out, token = together(*section_out, token)
    else:
        input_grad = rows_sent(grad_rows, me)
        g_fc = sum_fc.result()
    section_out, input_grad = [jnp.stack(straight(v, me)) for v in (section_out, input_grad)]
    g_out = sum_out.result()
    g_attn = [v.result() for v in sums_attn]
    g_attn = jnp.concatenate(g_attn, axis=1)

    g_attn, sums = g_attn[:-16], g_attn[-16:]
    g_wattn = g_attn[:, : 3 * width].reshape(-1, 3, width)
    g_wproj = g_attn[:, 3 * width :].T
    g_wout = g_out.T

    share = model // (groups * 4)
    g_bqv = sums[6, : 2 * width].reshape(2, width)
    g_bfc = sums[7]
    sums = lax.dynamic_slice_in_dim(sums, (lax.axis_index("dp") * 4 + me) * share, share, 1)
    return (
        section_out[None],
        input_grad[None],
        g_wattn[None],
        g_bqv[None],
        g_wproj[None],
        sums[4][None],
        g_fc[None],
        g_bfc[None],
        g_wout[None],
        sums[5][None],
        jnp.stack([sums[0], sums[2]])[None],
        jnp.stack([sums[1], sums[3]])[None],
    )


def solution(mesh):
    in_specs = (
        P(None, ("dp", "tensor"), None),
        P(None, ("dp", "tensor"), None),
        P("dp", None, None),
        P("section", None, None, "tensor"),
        P("section", None, "tensor"),
        P("section", "tensor", None),
        P("section", None),
        P("section", None, "tensor"),
        P("section", "tensor"),
        P("section", "tensor", None),
        P("section", None),
        P("section", None, None),
        P("section", None, None),
    )
    out_specs = (
        P("section", None, ("dp", "tensor"), None),
        P("section", None, ("dp", "tensor"), None),
        P("section", "dp", None, "tensor"),
        P("section", None, "tensor"),
        P("section", "tensor", "dp"),
        P("section", ("dp", "tensor")),
        P("section", "dp", "tensor"),
        P("section", "tensor"),
        P("section", "tensor", "dp"),
        P("section", ("dp", "tensor")),
        P("section", None, ("dp", "tensor")),
        P("section", None, ("dp", "tensor")),
    )
    return jax.shard_map(body, mesh=mesh, in_specs=in_specs, out_specs=out_specs, check_vma=False)
```
